256 devices in a mesh: seq: 32 (over z_hi, x, core), head: 8 (over z_lo, y).
Axes of the slice: x: 4, y: 4, z: 8 (z_hi: 4, z_lo: 2; z = z_hi * 2 + z_lo), core: 2. Of those that a mesh axis runs over, the one named last changes fastest.
Arguments:
- query: bfloat16 [16384, 5120], P(('seq', 'head')), may hold values from -15 to 15
- key_in: bfloat16 [16384, 5120], P(('seq', 'head')), may hold values from -15 to 15
- value: bfloat16 [16384, 5120], P(('seq', 'head')), may hold values from -6 to 6
- query_gain: float32 [5120], replicated, may hold values from 0.1 to 1.9
- key_gain: float32 [5120], replicated, may hold values from 0.1 to 1.9
- tile_lists: int32 [128, 20], replicated, may hold values from 0 to 127, as said below
- list_lengths: int32 [128], replicated, may hold values from 12 to 20
Outputs:
- attended: bfloat16 [16384, 5120], P(('seq', 'head'))
The draws below stay inside these ranges and needn't reach their ends.
Inputs may be any that keep to these rules, and one draw needn't show every extreme that they name: `tile_lists`: entries of row t past list_lengths[t] are 0. The first 4 entries of row t are the tiles g*4 to g*4 + 3 in order, g = t // 4; the further valid entries are distinct tiles outside that group. Over the 4 query tiles of one group, exactly 1 distinct tiles of every other group are listed.
All inputs are finite; a program needn't handle non-finite values.
Results may differ from the reference program's by a relative error of at most 0.012.
The reference program's roundings to bfloat16 on the way (of `query_norm`, `key_norm` and `weights`) count: a program that leaves them out, or rounds other values in their place, can miss the bound.
Values may be sent and summed in bfloat16 or wider, within the bound.
A program may use at most 128 MiB of HBM per device.

```python
import jax
import jax.numpy as jnp
from jax import lax

HEADS = 40
HD = 128
D = 5120
TILE = 128
CAP = 1
TOKENS = 16384
TPG = 4
NT = 128
REM = 16
REMMIN = 8
LIST = 20
N_SEQ = 32


def query_key_pair(key):
    base = jax.random.fold_in(key, 71)
    key_q, key_k = jax.random.split(base, 2)
    first = jax.random.truncated_normal(key_q, -3.0, 3.0, (TOKENS, D), jnp.float32)
    second = jax.random.truncated_normal(key_k, -3.0, 3.0, (TOKENS, D), jnp.float32)
    return (first, second)


def draw_query(key, part):
    return query_key_pair(key)[0].astype(jnp.bfloat16)


def draw_key_in(key, part):
    return query_key_pair(key)[1].astype(jnp.bfloat16)


def tile_plan(key):
    base = jax.random.fold_in(key, 19)
    key_pick, key_perm, key_level, key_top, key_drop, key_long = jax.random.split(base, 6)
    visible = (N_SEQ - 1) * CAP
    heaviest = jax.random.randint(key_long, (), 0, N_SEQ)

    def per_group(group):
        pick_keys = jax.random.split(jax.random.fold_in(key_pick, group), N_SEQ)
        picks = jax.vmap(lambda single: jax.random.permutation(single, TPG)[:CAP])(pick_keys)
        slot = jnp.arange(visible)
        source = slot // CAP
        source = source + (source >= group).astype(jnp.int32)
        column = slot % CAP
        pool_ids = source * TPG + picks[source, column]
        order = jax.random.permutation(jax.random.fold_in(key_perm, group), visible)
        level = jnp.minimum(jax.random.randint(jax.random.fold_in(key_level, group), (), 0, 8), 4)
        level = jnp.where(group == heaviest, 0, level)
        highest = REMMIN + jnp.right_shift(jnp.int32(REM - REMMIN), level)
        remote_count = jnp.maximum(REMMIN, highest - jax.random.randint(jax.random.fold_in(key_drop, group), (TPG,), 0, 3))
        longest = jax.random.randint(jax.random.fold_in(key_top, group), (), 0, TPG)
        remote_count = jnp.where(jnp.arange(TPG) == longest, highest, remote_count)
        offsets = jnp.cumsum(remote_count) - remote_count
        entry = jnp.arange(REM)
        position = (offsets[:, None] + entry[None, :]) % visible
        remote = jnp.where(entry[None, :] < remote_count[:, None], pool_ids[order[position]], 0)
        own = jnp.broadcast_to(group * TPG + jnp.arange(TPG)[None, :], (TPG, TPG))
        return (jnp.concatenate([own, remote], axis=1), TPG + remote_count)
    lists, counts = jax.vmap(per_group)(jnp.arange(N_SEQ))
    return (lists.reshape(NT, LIST).astype(jnp.int32), counts.reshape(NT).astype(jnp.int32))


def draw_tile_lists(key, part):
    return tile_plan(key)[0]


def draw_list_lengths(key, part):
    return tile_plan(key)[1]


def shard_levels(rng, dims, shards, low, top_value):
    def one(dim, blocks):
        heights = jax.random.uniform(jax.random.fold_in(jax.random.fold_in(rng, 6), dim), (blocks,), jnp.float32, low / len(shards), top_value / len(shards))
        return jnp.repeat(jnp.exp(heights), dims[dim] // blocks).reshape((-1,) + (1,) * (len(dims) - dim - 1))

    factor_of = one(*shards[0])
    for cut in shards[1:]:
        factor_of = factor_of * one(*cut)
    return factor_of


def scatter_about(own_key, dims, deviation, limit, shards=(), dtype=jnp.bfloat16):
    loudness = shard_levels(own_key, dims, shards, -0.22, 0.18) if shards else 1.0
    result = jax.random.normal(own_key, dims, jnp.float32) * deviation * loudness
    return jnp.minimum(jnp.maximum(result, -limit), limit).astype(dtype)


def setup_inputs(seed: int = 0) -> dict:
    seeds = jax.random.split(jax.random.key(seed), 8)
    query = draw_query(jax.random.fold_in(seeds[7], 71), 0)
    key_in = draw_key_in(jax.random.fold_in(seeds[7], 71), 0)
    value = scatter_about(seeds[2], (TOKENS, D), 1.0, 6.0, ((0, 256),))
    query_gain = jnp.clip(1.0 + 0.18 * jax.random.normal(seeds[3], (D,), jnp.float32), 0.1, 1.9)
    key_gain = jnp.clip(1.0 + 0.18 * jax.random.normal(seeds[4], (D,), jnp.float32), 0.1, 1.9)
    tile_lists = draw_tile_lists(jax.random.fold_in(seeds[7], 71), 0)
    list_lengths = draw_list_lengths(jax.random.fold_in(seeds[7], 71), 0)
    return dict(query=query, key_in=key_in, value=value, query_gain=query_gain, key_gain=key_gain, tile_lists=tile_lists, list_lengths=list_lengths)


def normalize(rows, gain):
    values = rows.astype(jnp.float32)
    square_mean = lax.optimization_barrier(jnp.mean(values * values, axis=1, keepdims=True))
    return (values * lax.rsqrt(square_mean + 1e-06) * gain).astype(jnp.bfloat16)

def reference(query, key_in, value, query_gain, key_gain, tile_lists, list_lengths):
    query_norm = normalize(query, query_gain)
    key_norm = normalize(key_in, key_gain)
    tile_total = TOKENS // TILE
    query_tiles = query_norm.reshape(tile_total, TILE, HEADS, HD)
    key_tiles = key_norm.reshape(tile_total, TILE, HEADS, HD)
    value_tiles = value.reshape(tile_total, TILE, HEADS, HD)
    scale = HD ** (-0.5)

    def one_tile(tile_no):
        tile_ids = tile_lists[tile_no].astype(jnp.int32)
        entry_count = list_lengths[tile_no]
        key_block = jnp.take(key_tiles, tile_ids, axis=0).reshape(LIST * TILE, HEADS, HD).astype(jnp.float32)
        value_block = jnp.take(value_tiles, tile_ids, axis=0).reshape(LIST * TILE, HEADS, HD).astype(jnp.float32)
        is_valid = jnp.repeat(jnp.arange(LIST) < entry_count, TILE)
        scores = jnp.einsum('qhd,khd->hqk', query_tiles[tile_no].astype(jnp.float32), key_block) * scale
        masked = jnp.where(is_valid[None, None, :], scores, -1e+30)
        rowmax = lax.optimization_barrier(jnp.max(masked, axis=-1, keepdims=True))
        raw = jnp.where(is_valid[None, None, :], jnp.exp(masked - rowmax), 0.0)
        total = lax.optimization_barrier(jnp.sum(raw, axis=-1))
        weights = lax.optimization_barrier(raw.astype(jnp.bfloat16)).astype(jnp.float32)
        mixed = jnp.einsum('hqk,khd->qhd', weights, value_block)
        return (mixed / jnp.transpose(total)[:, :, None]).astype(jnp.bfloat16)
    attended = lax.map(one_tile, jnp.arange(tile_total))
    return attended.reshape(TOKENS, D)
```

```python
import jax
import jax.numpy as jnp
from jax import lax
from jax.experimental import pallas as pl
from jax.experimental.pallas import tpu as pltpu
from jax.sharding import PartitionSpec as P

HD = 128
TILE = 128
HALF = 64
HEADS = 40
NX, NY, NZ, NC = 4, 4, 8, 2
SLICE = HEADS // NZ
LIST = 20
SURE = 12
UNITS = 20
BLOCKS = NC * NZ * NX
MESH = pl.DeviceIdType.MESH
OFFSETS = (0, 1, 7, 2, 6, 3, 5, 4)


def place():
    seq = lax.axis_index("seq")
    head = lax.axis_index("head")
    c = lax.rem(seq, 2)
    x = lax.rem(lax.div(seq, 2), NX)
    z_hi = lax.div(seq, 2 * NX)
    z_lo = lax.div(head, NY)
    y = lax.rem(head, NY)
    return x, y, 2 * z_hi + z_lo, c


def device(x, y, z, c):
    return ((lax.div(z, 2) * NX + x) * 2 + c, lax.rem(z, 2) * NY + y)


def send(src, dst, send_sem, recv_sem, target):
    pltpu.make_async_remote_copy(
        src_ref=src,
        dst_ref=dst,
        send_sem=send_sem,
        recv_sem=recv_sem,
        device_id=target,
        device_id_type=MESH,
    ).start()


def await_bytes(ref, sem):
    pltpu.make_async_copy(ref, ref, sem).wait()


def normalize_into(src, gain, dst_of_head):
    def rows(block, _):
        span = pl.ds(pl.multiple_of(block * 16, 16), 16)
        values = src[span, :].astype(jnp.float32)
        square_mean = jnp.mean(values * values, axis=1, keepdims=True)
        scale = lax.rsqrt(square_mean + 1e-06)
        for h in range(HEADS):
            cols = slice(h * HD, (h + 1) * HD)
            part = src[span, cols].astype(jnp.float32) * scale * gain[:, cols]
            dst_of_head(h, span, part.astype(jnp.bfloat16))
        return 0

    lax.fori_loop(0, HALF // 16, rows, 0)


def exchange_kernel(
    q_ref, k_ref, v_ref, qg_ref, kg_ref, row_kv, all_kv, queries,
    pack_kv, pack_q, z_send, x_send, y_send, mate_send, q_send,
    zr_recv, z4_recv, xr_recv, x4_recv, y4_recv, mate_recv, q_recv,
):
    x, y, z, c = place()
    barrier = pltpu.get_barrier_semaphore()
    partners = []
    for dz in range(NZ):
        for dy in range(NY):
            if dz or dy:
                partners.append(device(x, lax.rem(y + dy, NY), lax.rem(z + dz, NZ), c))
    right = device(lax.rem(x + 1, NX), y, z, c)
    left = device(lax.rem(x + NX - 1, NX), y, z, c)
    up = device(x, lax.rem(y + 1, NY), z, c)
    down = device(x, lax.rem(y + NY - 1, NY), z, c)
    mate = device(x, y, z, 1 - c)
    partners += [right, left, mate]
    for target in partners:
        pl.semaphore_signal(barrier, inc=1, device_id=target, device_id_type=MESH)

    def put_k(h, span, part):
        pack_kv[h, 0, span, :] = part

    def put_q(h, span, part):
        pack_q[h, span, :] = part

    normalize_into(k_ref, kg_ref, put_k)
    for h in range(HEADS):
        pack_kv[h, 1] = v_ref[:, h * HD:(h + 1) * HD]

    pl.semaphore_wait(barrier, len(partners))

    block = (c * NZ + z) * NX + x
    for i, dz in enumerate(OFFSETS):
        zd = lax.rem(z + dz, NZ)
        for dy in range(NY):
            yd = lax.rem(y + dy, NY)
            src = pack_kv.at[SLICE * zd + yd]
            dst = row_kv.at[block, :, y]
            if dz or dy:
                send(src, dst, z_send.at[0], zr_recv.at[i], device(x, yd, zd, c))
            else:
                pltpu.make_async_copy(src, dst, zr_recv.at[i]).start()
        src = pack_kv.at[SLICE * zd + NY]
        dst = all_kv.at[block, :, y]
        if dz:
            send(src, dst, z_send.at[0], z4_recv.at[i], device(x, y, zd, c))
        else:
            pltpu.make_async_copy(src, dst, z4_recv.at[i]).start()

    normalize_into(q_ref, qg_ref, put_q)
    z_hi, z_lo = lax.div(z, 2), lax.rem(z, 2)
    for i, dz in enumerate(OFFSETS):
        zd = lax.rem(z + dz, NZ)
        for dy in range(NY):
            yd = lax.rem(y + dy, NY)
            src = pack_q.at[SLICE * zd + yd]
            dst = queries.at[z * NY + y]
            if dz or dy:
                send(src, dst, q_send.at[0], q_recv.at[0], device(x, yd, zd, c))
            else:
                pltpu.make_async_copy(src, dst, q_recv.at[0]).start()
        src = pack_q.at[SLICE * zd + NY]
        dst = queries.at[NZ * NY + z_lo * NY + y]
        if dz:
            send(src, dst, q_send.at[0], q_recv.at[0], device(x, z_hi, zd, c))
        else:
            @pl.when(z_hi == y)
            def _(src=src, dst=dst):
                pltpu.make_async_copy(src, dst, q_recv.at[0]).start()

            @pl.when(z_hi != y)
            def _(src=src, dst=dst, zd=zd):
                send(src, dst, q_send.at[1], q_recv.at[0], device(x, z_hi, zd, c))

    x_left, x_right, x_far = lax.rem(x + NX - 1, NX), lax.rem(x + 1, NX), lax.rem(x + 2, NX)
    y_down, y_up, y_far = lax.rem(y + NY - 1, NY), lax.rem(y + 1, NY), lax.rem(y + 2, NY)

    def first(i):
        return (c * NZ + lax.rem(z + NZ - OFFSETS[i], NZ)) * NX

    def own_along_x(i):
        mine = row_kv.at[first(i) + x]
        await_bytes(mine, zr_recv.at[i])
        send(mine, mine, x_send.at[0], xr_recv.at[0, i], right)
        send(mine, mine, x_send.at[0], xr_recv.at[1, i], left)
        mine = all_kv.at[first(i) + x, :, y]
        await_bytes(mine, z4_recv.at[i])
        send(mine, mine, x_send.at[1], x4_recv.at[0, i], right)
        send(mine, mine, x_send.at[1], x4_recv.at[1, i], left)

    def far_along_x(i):
        from_left = row_kv.at[first(i) + x_left]
        from_right = row_kv.at[first(i) + x_right]
        await_bytes(from_left, xr_recv.at[0, i])
        await_bytes(from_right, xr_recv.at[1, i])
        if i % 2 == 0:
            send(from_left, from_left, x_send.at[0], xr_recv.at[2, i], right)
        else:
            send(from_right, from_right, x_send.at[0], xr_recv.at[2, i], left)
        from_left = all_kv.at[first(i) + x_left, :, y]
        from_right = all_kv.at[first(i) + x_right, :, y]
        await_bytes(from_left, x4_recv.at[0, i])
        await_bytes(from_right, x4_recv.at[1, i])
        if i % 2 == 0:
            send(from_left, from_left, x_send.at[1], x4_recv.at[2, i], right)
        else:
            send(from_right, from_right, x_send.at[1], x4_recv.at[2, i], left)

    def own_along_y(i):
        await_bytes(all_kv.at[first(i) + x_far, :, y], x4_recv.at[2, i])
        mine = all_kv.at[pl.ds(first(i), NX), :, y]
        send(mine, mine, y_send.at[0], y4_recv.at[0, i], up)
        send(mine, mine, y_send.at[0], y4_recv.at[1, i], down)
        await_bytes(row_kv.at[first(i) + x_far], xr_recv.at[2, i])
        whole = row_kv.at[pl.ds(first(i), NX)]
        send(whole, whole, mate_send.at[0], mate_recv.at[0], mate)

    def far_along_y(i):
        from_down = all_kv.at[pl.ds(first(i), NX), :, y_down]
        from_up = all_kv.at[pl.ds(first(i), NX), :, y_up]
        await_bytes(from_down, y4_recv.at[0, i])
        await_bytes(from_up, y4_recv.at[1, i])
        if i % 2 == 0:
            send(from_down, from_down, y_send.at[0], y4_recv.at[2, i], up)
        else:
            send(from_up, from_up, y_send.at[0], y4_recv.at[2, i], down)

    def to_mate(i):
        await_bytes(all_kv.at[pl.ds(first(i), NX), :, y_far], y4_recv.at[2, i])
        whole = all_kv.at[pl.ds(first(i), NX)]
        send(whole, whole, mate_send.at[1], mate_recv.at[1], mate)

    stages = ((6, to_mate), (5, far_along_y), (3, own_along_y), (2, far_along_x), (0, own_along_x))
    for step in range(NZ + 6):
        for lag, stage in stages:
            if 0 <= step - lag < NZ:
                stage(step - lag)

    other = row_kv.at[pl.ds((1 - c) * NZ * NX, NZ * NX)]
    await_bytes(other, mate_recv.at[0])
    other = all_kv.at[pl.ds((1 - c) * NZ * NX, NZ * NX)]
    await_bytes(other, mate_recv.at[1])
    await_bytes(queries, q_recv.at[0])

    await_bytes(pack_kv.at[pl.ds(0, NZ * NY - 1 + NZ - 1)], z_send.at[0])
    await_bytes(pack_q.at[pl.ds(0, NZ * NY - 1 + NZ - 1)], q_send.at[0])

    @pl.when(z_hi != y)
    def _():
        await_bytes(pack_q.at[0], q_send.at[1])

    await_bytes(row_kv.at[pl.ds(0, 3 * NZ)], x_send.at[0])
    await_bytes(all_kv.at[pl.ds(0, 3 * NZ), :, 0], x_send.at[1])
    await_bytes(all_kv.at[pl.ds(0, 3 * NZ)], y_send.at[0])
    await_bytes(row_kv.at[pl.ds(0, NX * NZ)], mate_send.at[0])
    await_bytes(all_kv.at[pl.ds(0, NX * NZ)], mate_send.at[1])


def exchange(query, key_in, value, query_gain, key_gain):
    kv_type = jax.ShapeDtypeStruct((BLOCKS, 2, NY, HALF, HD), jnp.bfloat16)
    q_type = jax.ShapeDtypeStruct((2 * UNITS, HALF, HD), jnp.bfloat16)
    vmem = pl.BlockSpec(memory_space=pltpu.VMEM)
    hbm = pl.BlockSpec(memory_space=pl.ANY)
    dma = pltpu.SemaphoreType.DMA
    return pl.pallas_call(
        exchange_kernel,
        out_shape=(kv_type, kv_type, q_type),
        in_specs=[vmem] * 5,
        out_specs=(hbm, hbm, hbm),
        scratch_shapes=[
            pltpu.VMEM((HEADS, 2, HALF, HD), jnp.bfloat16),
            pltpu.VMEM((HEADS, HALF, HD), jnp.bfloat16),
            dma((1,)), dma((2,)), dma((1,)), dma((2,)), dma((2,)),
            dma((NZ,)), dma((NZ,)), dma((3, NZ)), dma((3, NZ)), dma((3, NZ)), dma((2,)), dma((1,)),
        ],
        compiler_params=pltpu.CompilerParams(
            collective_id=0, has_side_effects=True, vmem_limit_bytes=32 * 2**20
        ),
        name="exchange",
    )(query, key_in, value, query_gain.reshape(1, -1), key_gain.reshape(1, -1))


def attend_kernel(lists, lengths, row_kv, all_kv, q_ref, out_ref, scores):
    x, y, z, c = place()
    scale = HD ** (-0.5)

    def unit(kv, u, group_tile):
        length = lengths[group_tile]
        q_tile = q_ref[u]

        def tile_at(n):
            entry = lists[n, group_tile]
            z = ((entry >> 5) << 1) + ((entry >> 1) & 1)
            block = ((((entry >> 2) & 1) * NZ) + z) * NX + ((entry >> 3) & 3)
            return block, entry & 1

        def score(n):
            block, a = tile_at(n)
            keys = kv[block, 0, a]
            return lax.dot_general(
                q_tile, keys, (((1,), (1,)), ((), ())), preferred_element_type=jnp.float32
            )

        high = None
        for n in range(SURE):
            s = score(n)
            scores[n] = s
            high = s if high is None else jnp.maximum(high, s)
        scores_high = high

        def more_scores(n, high):
            s = score(n)
            scores[n] = s
            return jnp.maximum(high, s)

        high = lax.fori_loop(SURE, length, more_scores, scores_high)
        row_high = jnp.max(high, axis=1, keepdims=True) * scale

        def weigh(n, total, acc):
            block, a = tile_at(n)
            raw = jnp.exp(scores[n] * scale - row_high)
            mixed = jnp.dot(
                raw.astype(jnp.bfloat16), kv[block, 1, a],
                preferred_element_type=jnp.float32,
            )
            return total + raw, acc + mixed

        total = jnp.zeros((TILE, TILE), jnp.float32)
        acc = jnp.zeros((TILE, HD), jnp.float32)
        for n in range(SURE):
            total, acc = weigh(n, total, acc)
        total, acc = lax.fori_loop(
            SURE, length, lambda n, state: weigh(n, *state), (total, acc)
        )
        summed = jnp.sum(total, axis=1, keepdims=True)
        out_ref[u] = (acc / summed).astype(jnp.bfloat16)

    def row_unit(u, _):
        unit(row_kv, u, (((u >> 2) * NX + x) * 2 + c) * 4 + (u & 3))
        return 0

    lax.fori_loop(0, 16, row_unit, 0)

    def all_unit(v, _):
        unit(all_kv, 16 + v, ((y * NX + x) * 2 + c) * 4 + v)
        return 0

    lax.fori_loop(0, 4, all_unit, 0)


def attend(row_kv, all_kv, queries, tile_lists, list_lengths):
    smem = pl.BlockSpec(memory_space=pltpu.SMEM)
    vmem = pl.BlockSpec(memory_space=pltpu.VMEM)
    shape = (BLOCKS, 2, 2, TILE, HD)
    return pl.pallas_call(
        attend_kernel,
        out_shape=jax.ShapeDtypeStruct((UNITS, TILE, HD), jnp.bfloat16),
        in_specs=[smem, smem, vmem, vmem, vmem],
        out_specs=vmem,
        scratch_shapes=[
            pltpu.VMEM((LIST, TILE, TILE), jnp.float32),
        ],
        compiler_params=pltpu.CompilerParams(vmem_limit_bytes=24 * 2**20),
        name="attend",
    )(
        tile_lists.T, list_lengths,
        row_kv.reshape(shape), all_kv.reshape(shape), queries.reshape(UNITS, TILE, HD),
    )


def return_kernel(o_ref, out_ref, send_sem, recv_sem):
    x, y, z, c = place()
    barrier = pltpu.get_barrier_semaphore()
    count = 0
    for dz in range(NZ):
        for dy in range(NY):
            if dz or dy:
                target = device(x, lax.rem(y + dy, NY), lax.rem(z + dz, NZ), c)
                pl.semaphore_signal(barrier, inc=1, device_id=target, device_id_type=MESH)
                count += 1
    pl.semaphore_wait(barrier, count)

    columns = out_ref.at[:, pl.ds(pl.multiple_of((SLICE * z + y) * HD, HD), HD)]
    for dz in OFFSETS:
        zd = lax.rem(z + dz, NZ)
        for dy in range(NY):
            yd = lax.rem(y + dy, NY)
            src = o_ref.at[zd * NY + yd]
            if dz or dy:
                send(src, columns, send_sem.at[0], recv_sem.at[0], device(x, yd, zd, c))
            else:
                pltpu.make_async_copy(src, columns, recv_sem.at[0]).start()
    columns = out_ref.at[:, pl.ds(pl.multiple_of((SLICE * z + NY) * HD, HD), HD)]
    for z_lo in range(2):
        zd = 2 * y + z_lo
        for dy in range(NY):
            yd = lax.rem(y + dy, NY)
            src = o_ref.at[NZ * NY + z_lo * NY + yd]
            if dy:
                send(src, columns, send_sem.at[0], recv_sem.at[0], device(x, yd, zd, c))
            else:
                @pl.when(zd == z)
                def _(src=src):
                    pltpu.make_async_copy(src, columns, recv_sem.at[0]).start()

                @pl.when(zd != z)
                def _(src=src, yd=yd, zd=zd, z_lo=z_lo):
                    send(src, columns, send_sem.at[1 + z_lo], recv_sem.at[0], device(x, yd, zd, c))

    await_bytes(out_ref, recv_sem.at[0])
    await_bytes(o_ref.at[pl.ds(0, NZ * NY - 1 + 2 * (NY - 1))], send_sem.at[0])
    for z_lo in range(2):
        @pl.when(2 * y + z_lo != z)
        def _(z_lo=z_lo):
            await_bytes(o_ref.at[0], send_sem.at[1 + z_lo])


def give_back(attended):
    hbm = pl.BlockSpec(memory_space=pl.ANY)
    dma = pltpu.SemaphoreType.DMA
    return pl.pallas_call(
        return_kernel,
        out_shape=jax.ShapeDtypeStruct((HALF, HEADS * HD), jnp.bfloat16),
        in_specs=[pl.BlockSpec(memory_space=pltpu.VMEM)],
        out_specs=hbm,
        scratch_shapes=[dma((3,)), dma((1,))],
        compiler_params=pltpu.CompilerParams(
            collective_id=1, has_side_effects=True, vmem_limit_bytes=8 * 2**20
        ),
        name="give_back",
    )(attended.reshape(2 * UNITS, HALF, HD))


def local(query, key_in, value, query_gain, key_gain, tile_lists, list_lengths):
    row_kv, all_kv, queries = exchange(query, key_in, value, query_gain, key_gain)
    attended = attend(row_kv, all_kv, queries, tile_lists, list_lengths)
    return give_back(attended)


def solution(mesh):
    in_specs = (
        P(("seq", "head"), None),
        P(("seq", "head"), None),
        P(("seq", "head"), None),
        P(),
        P(),
        P(),
        P(),
    )
    out_specs = P(("seq", "head"), None)
    return jax.shard_map(local, mesh=mesh, in_specs=in_specs, out_specs=out_specs, check_vma=False)
```

```python
import math

import jax
import jax.numpy as jnp
from jax import lax
from jax.experimental import pallas as pl
from jax.experimental.pallas import tpu as pltpu
from jax.sharding import PartitionSpec as P

HD = 128
TILE = 128
HALF = 64
HEADS = 40
NX, NY, NZ, NC = 4, 4, 8, 2
SLICE = HEADS // NZ
LIST = 20
SURE = 12
PAIR = 2
LOG2_SCALE = HD ** (-0.5) * math.log2(math.e)
UNITS = 20
BLOCKS = NC * NZ * NX
MESH = pl.DeviceIdType.MESH
OFFSETS = (0, 1, 7, 2, 6, 3, 5, 4)


def place():
    seq = lax.axis_index("seq")
    head = lax.axis_index("head")
    c = lax.rem(seq, 2)
    x = lax.rem(lax.div(seq, 2), NX)
    z_hi = lax.div(seq, 2 * NX)
    z_lo = lax.div(head, NY)
    y = lax.rem(head, NY)
    return x, y, 2 * z_hi + z_lo, c


def device(x, y, z, c):
    return ((lax.div(z, 2) * NX + x) * 2 + c, lax.rem(z, 2) * NY + y)


def send(src, dst, send_sem, recv_sem, target):
    pltpu.make_async_remote_copy(
        src_ref=src,
        dst_ref=dst,
        send_sem=send_sem,
        recv_sem=recv_sem,
        device_id=target,
        device_id_type=MESH,
    ).start()


def await_bytes(ref, sem):
    pltpu.make_async_copy(ref, ref, sem).wait()


def normalize_into(src, gain, dst_of_head):
    def rows(block, _):
        span = pl.ds(pl.multiple_of(block * 16, 16), 16)
        squares = jnp.zeros((16, HD), jnp.float32)
        for h in range(HEADS):
            part = src[span, h * HD:(h + 1) * HD].astype(jnp.float32)
            squares = squares + part * part
        square_mean = jnp.sum(squares, axis=1, keepdims=True) * (1.0 / (HEADS * HD))
        scale = lax.rsqrt(square_mean + 1e-06)
        for h in range(HEADS):
            cols = slice(h * HD, (h + 1) * HD)
            part = src[span, cols].astype(jnp.float32) * scale * gain[:, cols]
            dst_of_head(h, span, part.astype(jnp.bfloat16))
        return 0

    lax.fori_loop(0, HALF // 16, rows, 0)


def attend_unit(kv, q_tile, out_ref, out_index, lists, row, length, scores):
    at = []
    for n in range(LIST):
        entry = lists[n, row]
        z = ((entry >> 5) << 1) + ((entry >> 1) & 1)
        at.append(((((entry >> 2) & 1) * NZ + z) * NX + ((entry >> 3) & 3), entry & 1))
    high = None
    for n in range(0, LIST, PAIR):
        keys = jnp.concatenate(
            [kv[at[m][0], 0, pl.ds(2 * at[m][1], 2)].reshape(TILE, HD) for m in range(n, n + PAIR)], axis=0
        )
        both = lax.dot_general(
            q_tile, keys, (((1,), (1,)), ((), ())), preferred_element_type=jnp.float32
        )
        for m in range(n, n + PAIR):
            s = both[:, (m - n) * TILE:(m - n + 1) * TILE]
            if m >= SURE:
                s = jnp.where(m < length, s, -1e30)
            scores[m] = s
            high = s if high is None else jnp.maximum(high, s)
    row_high = jnp.max(high, axis=1, keepdims=True)
    total = None
    acc = None
    for n in range(0, LIST, PAIR):
        weights = []
        for m in range(n, n + PAIR):
            raw = jnp.exp2((scores[m] - row_high) * LOG2_SCALE)
            total = raw if total is None else total + raw
            weights.append(raw.astype(jnp.bfloat16))
        values = jnp.concatenate(
            [kv[at[m][0], 1, pl.ds(2 * at[m][1], 2)].reshape(TILE, HD) for m in range(n, n + PAIR)], axis=0
        )
        mixed = jnp.dot(
            jnp.concatenate(weights, axis=1), values, preferred_element_type=jnp.float32
        )
        acc = mixed if acc is None else acc + mixed
    summed = jnp.sum(total, axis=1, keepdims=True)
    out_ref[out_index] = (acc / summed).astype(jnp.bfloat16).reshape(2, HALF, HD)


def fused_kernel(
    q_hbm, k_hbm, v_hbm, qg_hbm, kg_hbm, lists_hbm, lengths_hbm, out_ref,
    q_ref, k_ref, v_ref, qg_ref, kg_ref, lists, lengths,
    pack_kv, pack_q, row_kv, all_kv, queries, scores, results,
    load_sem, z_send, x_send, y_send, mate_send, q_send, out_send,
    zr_recv, z4_recv, xr_recv, x4_recv, y4_recv, mate_recv, q_recv, out_recv,
):
    loads = []
    for n, (src, dst) in enumerate((
        (k_hbm, k_ref), (kg_hbm, kg_ref), (v_hbm, v_ref), (q_hbm, q_ref), (qg_hbm, qg_ref),
        (lists_hbm, lists), (lengths_hbm, lengths),
    )):
        copy = pltpu.make_async_copy(src, dst, load_sem.at[n])
        copy.start()
        loads.append(copy)
    x, y, z, c = place()
    barrier = pltpu.get_barrier_semaphore()
    partners = []
    for dz in range(NZ):
        for dy in range(NY):
            if dz or dy:
                partners.append(device(x, lax.rem(y + dy, NY), lax.rem(z + dz, NZ), c))
    right = device(lax.rem(x + 1, NX), y, z, c)
    left = device(lax.rem(x + NX - 1, NX), y, z, c)
    up = device(x, lax.rem(y + 1, NY), z, c)
    down = device(x, lax.rem(y + NY - 1, NY), z, c)
    mate = device(x, y, z, 1 - c)
    partners += [right, left, mate]
    for target in partners:
        pl.semaphore_signal(barrier, inc=1, device_id=target, device_id_type=MESH)

    def put_k(h, span, part):
        pack_kv[h, 0, span, :] = part

    def put_q(h, span, part):
        pack_q[h, span, :] = part

    loads[0].wait()
    loads[1].wait()
    normalize_into(k_ref, kg_ref, put_k)
    loads[2].wait()
    for h in range(HEADS):
        pack_kv[h, 1] = v_ref[:, h * HD:(h + 1) * HD]

    pl.semaphore_wait(barrier, len(partners))

    block = (c * NZ + z) * NX + x
    for i, dz in enumerate(OFFSETS):
        zd = lax.rem(z + dz, NZ)
        for dy in range(NY):
            yd = lax.rem(y + dy, NY)
            src = pack_kv.at[SLICE * zd + yd]
            dst = row_kv.at[block, :, y]
            if dz or dy:
                send(src, dst, z_send.at[0], zr_recv.at[i], device(x, yd, zd, c))
            else:
                pltpu.make_async_copy(src, dst, zr_recv.at[i]).start()
        src = pack_kv.at[SLICE * zd + NY]
        dst = all_kv.at[block, :, y]
        if dz:
            send(src, dst, z_send.at[0], z4_recv.at[i], device(x, y, zd, c))
        else:
            pltpu.make_async_copy(src, dst, z4_recv.at[i]).start()

    loads[3].wait()
    loads[4].wait()
    normalize_into(q_ref, qg_ref, put_q)
    z_hi, z_lo = lax.div(z, 2), lax.rem(z, 2)
    for i, dz in enumerate(OFFSETS):
        zd = lax.rem(z + dz, NZ)
        for dy in range(NY):
            yd = lax.rem(y + dy, NY)
            src = pack_q.at[SLICE * zd + yd]
            dst = queries.at[z * NY + y]
            if dz or dy:
                send(src, dst, q_send.at[0], q_recv.at[0], device(x, yd, zd, c))
            else:
                pltpu.make_async_copy(src, dst, q_recv.at[0]).start()
        src = pack_q.at[SLICE * zd + NY]
        dst = queries.at[NZ * NY + z_lo * NY + y]
        if dz:
            send(src, dst, q_send.at[0], q_recv.at[0], device(x, z_hi, zd, c))
        else:
            @pl.when(z_hi == y)
            def _(src=src, dst=dst):
                pltpu.make_async_copy(src, dst, q_recv.at[0]).start()

            @pl.when(z_hi != y)
            def _(src=src, dst=dst, zd=zd):
                send(src, dst, q_send.at[1], q_recv.at[0], device(x, z_hi, zd, c))

    x_left, x_right, x_far = lax.rem(x + NX - 1, NX), lax.rem(x + 1, NX), lax.rem(x + 2, NX)
    y_down, y_up, y_far = lax.rem(y + NY - 1, NY), lax.rem(y + 1, NY), lax.rem(y + 2, NY)

    def first(i):
        return (c * NZ + lax.rem(z + NZ - OFFSETS[i], NZ)) * NX

    def own_along_x(i):
        mine = row_kv.at[first(i) + x]
        await_bytes(mine, zr_recv.at[i])
        send(mine, mine, x_send.at[0], xr_recv.at[0, i], right)
        send(mine, mine, x_send.at[0], xr_recv.at[1, i], left)

    def far_along_x(i):
        from_left = row_kv.at[first(i) + x_left]
        from_right = row_kv.at[first(i) + x_right]
        await_bytes(from_left, xr_recv.at[0, i])
        await_bytes(from_right, xr_recv.at[1, i])
        if i % 2 == 0:
            send(from_left, from_left, x_send.at[0], xr_recv.at[2, i], right)
        else:
            send(from_right, from_right, x_send.at[0], xr_recv.at[2, i], left)

    def to_mate(i):
        await_bytes(row_kv.at[first(i) + x_far], xr_recv.at[2, i])
        whole = row_kv.at[pl.ds(first(i), NX)]
        send(whole, whole, mate_send.at[0], mate_recv.at[0], mate)

    def own_along_x4(i):
        mine = all_kv.at[first(i) + x, :, y]
        await_bytes(mine, z4_recv.at[i])
        send(mine, mine, x_send.at[1], x4_recv.at[0, i], right)
        send(mine, mine, x_send.at[1], x4_recv.at[1, i], left)

    def far_along_x4(i):
        from_left = all_kv.at[first(i) + x_left, :, y]
        from_right = all_kv.at[first(i) + x_right, :, y]
        await_bytes(from_left, x4_recv.at[0, i])
        await_bytes(from_right, x4_recv.at[1, i])
        if i % 2 == 0:
            send(from_left, from_left, x_send.at[1], x4_recv.at[2, i], right)
        else:
            send(from_right, from_right, x_send.at[1], x4_recv.at[2, i], left)

    def own_along_y4(i):
        await_bytes(all_kv.at[first(i) + x_far, :, y], x4_recv.at[2, i])
        mine = all_kv.at[pl.ds(first(i), NX), :, y]
        send(mine, mine, y_send.at[0], y4_recv.at[0, i], up)
        send(mine, mine, y_send.at[0], y4_recv.at[1, i], down)

    def far_along_y4(i):
        from_down = all_kv.at[pl.ds(first(i), NX), :, y_down]
        from_up = all_kv.at[pl.ds(first(i), NX), :, y_up]
        await_bytes(from_down, y4_recv.at[0, i])
        await_bytes(from_up, y4_recv.at[1, i])
        if i % 2 == 0:
            send(from_down, from_down, y_send.at[0], y4_recv.at[2, i], up)
        else:
            send(from_up, from_up, y_send.at[0], y4_recv.at[2, i], down)

    def to_mate4(i):
        await_bytes(all_kv.at[pl.ds(first(i), NX), :, y_far], y4_recv.at[2, i])
        whole = all_kv.at[pl.ds(first(i), NX)]
        send(whole, whole, mate_send.at[1], mate_recv.at[1], mate)

    row_stages = ((3, to_mate), (2, far_along_x), (0, own_along_x))
    all_stages = ((6, to_mate4), (5, far_along_y4), (3, own_along_y4), (2, far_along_x4), (0, own_along_x4))

    def run(stages, step):
        for lag, stage in stages:
            if 0 <= step - lag < NZ:
                stage(step - lag)

    row_steps = NZ + 3
    for step in range(row_steps):
        run(all_stages, step)
        run(row_stages, step)

    loads[5].wait()
    loads[6].wait()
    await_bytes(queries, q_recv.at[0])
    await_bytes(row_kv.at[pl.ds((1 - c) * NZ * NX, NZ * NX)], mate_recv.at[0])

    columns = out_ref.at[:, pl.ds(pl.multiple_of((SLICE * z + y) * HD, HD), HD)]
    columns4 = out_ref.at[:, pl.ds(pl.multiple_of((SLICE * z + NY) * HD, HD), HD)]

    def row_unit(u, _):
        for t in range(NZ + 6 - row_steps):
            @pl.when(u == 2 * t + 1)
            def _(t=t):
                run(all_stages, row_steps + t)

        k, a = lax.div(u, 2), lax.rem(u, 2)
        odd = lax.rem(k, 2)
        zd = lax.rem(z + NY + lax.div(k + odd, 2) * (2 * odd - 1), NZ)
        row = ((lax.div(zd, 2) * NX + x) * 2 + c) * 4 + lax.rem(zd, 2) * 2 + a
        mine = zd * 2 + a
        q_tile = queries[pl.ds(2 * mine, 2)].reshape(TILE, HD)
        attend_unit(row_kv, q_tile, results, mine, lists, row, lengths[row], scores)
        for half in range(2):
            yd = 2 * a + half
            src = results.at[mine, half]

            @pl.when((zd == z) & (yd == y))
            def _(src=src):
                pltpu.make_async_copy(src, columns, out_recv.at[0]).start()

            @pl.when((zd != z) | (yd != y))
            def _(src=src, yd=yd):
                send(src, columns, out_send.at[0], out_recv.at[0], device(x, yd, zd, c))
        return 0

    lax.fori_loop(0, NZ * 2, row_unit, 0)
    await_bytes(all_kv.at[pl.ds((1 - c) * NZ * NX, NZ * NX)], mate_recv.at[1])

    def all_unit(v, _):
        row = ((y * NX + x) * 2 + c) * 4 + v
        mine = NZ * 2 + v
        q_tile = queries[pl.ds(2 * mine, 2)].reshape(TILE, HD)
        attend_unit(all_kv, q_tile, results, mine, lists, row, lengths[row], scores)
        zd = 2 * y + lax.div(v, 2)
        for half in range(2):
            yd = 2 * lax.rem(v, 2) + half
            src = results.at[mine, half]

            @pl.when((zd == z) & (yd == y))
            def _(src=src):
                pltpu.make_async_copy(src, columns4, out_recv.at[0]).start()

            @pl.when((zd != z) | (yd != y))
            def _(src=src, yd=yd):
                send(src, columns4, out_send.at[1], out_recv.at[0], device(x, yd, zd, c))
        return 0

    lax.fori_loop(0, NY, all_unit, 0)

    await_bytes(pack_kv.at[pl.ds(0, NZ * NY - 1 + NZ - 1)], z_send.at[0])
    await_bytes(pack_q.at[pl.ds(0, NZ * NY - 1 + NZ - 1)], q_send.at[0])

    @pl.when(z_hi != y)
    def _():
        await_bytes(pack_q.at[0], q_send.at[1])
        await_bytes(pack_q.at[pl.ds(0, 2 * NY)], out_send.at[1])

    @pl.when(z_hi == y)
    def _():
        await_bytes(pack_q.at[pl.ds(0, 2 * NY - 1)], out_send.at[1])

    await_bytes(row_kv.at[pl.ds(0, 3 * NZ)], x_send.at[0])
    await_bytes(all_kv.at[pl.ds(0, 3 * NZ), :, 0], x_send.at[1])
    await_bytes(all_kv.at[pl.ds(0, 3 * NZ)], y_send.at[0])
    await_bytes(row_kv.at[pl.ds(0, NX * NZ)], mate_send.at[0])
    await_bytes(all_kv.at[pl.ds(0, NX * NZ)], mate_send.at[1])
    await_bytes(pack_q.at[pl.ds(0, NZ * NY - 1)], out_send.at[0])
    await_bytes(out_ref, out_recv.at[0])


def local(query, key_in, value, query_gain, key_gain, tile_lists, list_lengths):
    rows, width = query.shape
    listed = tile_lists.T
    bf16 = jnp.bfloat16
    hbm = pl.BlockSpec(memory_space=pl.ANY)
    dma = pltpu.SemaphoreType.DMA
    return pl.pallas_call(
        fused_kernel,
        out_shape=jax.ShapeDtypeStruct((rows, width), bf16),
        in_specs=[hbm] * 7,
        out_specs=hbm,
        scratch_shapes=[
            pltpu.VMEM((rows, width), bf16),
            pltpu.VMEM((rows, width), bf16),
            pltpu.VMEM((rows, width), bf16),
            pltpu.VMEM((1, width), jnp.float32),
            pltpu.VMEM((1, width), jnp.float32),
            pltpu.SMEM(listed.shape, jnp.int32),
            pltpu.SMEM(list_lengths.shape, jnp.int32),
            pltpu.VMEM((HEADS, 2, HALF, HD), bf16),
            pltpu.VMEM((HEADS, HALF, HD), bf16),
            pltpu.VMEM((BLOCKS, 2, NY, HALF, HD), bf16),
            pltpu.VMEM((BLOCKS, 2, NY, HALF, HD), bf16),
            pltpu.VMEM((2 * UNITS, HALF, HD), bf16),
            pltpu.VMEM((LIST, TILE, TILE), jnp.float32),
            pltpu.VMEM((UNITS, 2, HALF, HD), bf16),
            dma((7,)), dma((1,)), dma((2,)), dma((1,)), dma((2,)), dma((2,)), dma((2,)),
            dma((NZ,)), dma((NZ,)), dma((3, NZ)), dma((3, NZ)), dma((3, NZ)), dma((2,)), dma((1,)), dma((1,)),
        ],
        compiler_params=pltpu.CompilerParams(
            collective_id=0, has_side_effects=True, vmem_limit_bytes=56 * 2**20
        ),
        name="fused",
    )(
        query, key_in, value, query_gain.reshape(1, -1), key_gain.reshape(1, -1),
        listed, list_lengths,
    )


def solution(mesh):
    in_specs = (
        P(("seq", "head"), None),
        P(("seq", "head"), None),
        P(("seq", "head"), None),
        P(),
        P(),
        P(),
        P(),
    )
    out_specs = P(("seq", "head"), None)
    return jax.shard_map(local, mesh=mesh, in_specs=in_specs, out_specs=out_specs, check_vma=False)
```

```python
import math

import jax
import jax.numpy as jnp
from jax import lax
from jax.experimental import pallas as pl
from jax.experimental.pallas import tpu as pltpu
from jax.sharding import PartitionSpec as P

HD = 128
TILE = 128
HALF = 64
HEADS = 40
NX, NY, NZ, NC = 4, 4, 8, 2
SLICE = HEADS // NZ
LIST = 20
SURE = 12
PAIR = 2
LOG2_SCALE = HD ** (-0.5) * math.log2(math.e)
UNITS = 20
BLOCKS = NC * NZ * NX
MESH = pl.DeviceIdType.MESH
COMBINE_AT = 8
ROW_DELAY = 4
PART_UNITS = {12: 4, 13: 3, 14: 3, 15: 3, 16: 3}
OFFSETS = (0, 1, 7, 2, 6, 3, 5, 4)


def place():
    seq = lax.axis_index("seq")
    head = lax.axis_index("head")
    c = lax.rem(seq, 2)
    x = lax.rem(lax.div(seq, 2), NX)
    z_hi = lax.div(seq, 2 * NX)
    z_lo = lax.div(head, NY)
    y = lax.rem(head, NY)
    return x, y, 2 * z_hi + z_lo, c


def device(x, y, z, c):
    return ((lax.div(z, 2) * NX + x) * 2 + c, lax.rem(z, 2) * NY + y)


def send(src, dst, send_sem, recv_sem, target):
    pltpu.make_async_remote_copy(
        src_ref=src,
        dst_ref=dst,
        send_sem=send_sem,
        recv_sem=recv_sem,
        device_id=target,
        device_id_type=MESH,
    ).start()


def await_bytes(ref, sem):
    pltpu.make_async_copy(ref, ref, sem).wait()


def normalize_into(src, gain, dst_of_head):
    def rows(block, _):
        span = pl.ds(pl.multiple_of(block * 16, 16), 16)
        squares = jnp.zeros((16, HD), jnp.float32)
        for h in range(HEADS):
            part = src[span, h * HD:(h + 1) * HD].astype(jnp.float32)
            squares = squares + part * part
        square_mean = jnp.sum(squares, axis=1, keepdims=True) * (1.0 / (HEADS * HD))
        scale = lax.rsqrt(square_mean + 1e-06)
        for h in range(HEADS):
            cols = slice(h * HD, (h + 1) * HD)
            part = src[span, cols].astype(jnp.float32) * scale * gain[:, cols]
            dst_of_head(h, span, part.astype(jnp.bfloat16))
        return 0

    lax.fori_loop(0, HALF // 16, rows, 0)


def attend_unit(kv, q_tile, out_ref, out_index, lists, row, length, scores):
    at = []
    for n in range(LIST):
        entry = lists[n, row]
        z = ((entry >> 5) << 1) + ((entry >> 1) & 1)
        at.append(((((entry >> 2) & 1) * NZ + z) * NX + ((entry >> 3) & 3), entry & 1))
    high = None
    for n in range(0, LIST, PAIR):
        keys = jnp.concatenate(
            [kv[at[m][0], 0, pl.ds(2 * at[m][1], 2)].reshape(TILE, HD) for m in range(n, n + PAIR)], axis=0
        )
        both = lax.dot_general(
            q_tile, keys, (((1,), (1,)), ((), ())), preferred_element_type=jnp.float32
        )
        for m in range(n, n + PAIR):
            s = both[:, (m - n) * TILE:(m - n + 1) * TILE]
            if m >= SURE:
                s = jnp.where(m < length, s, -1e30)
            scores[m] = s
            high = s if high is None else jnp.maximum(high, s)
    row_high = jnp.max(high, axis=1, keepdims=True)
    total = None
    acc = None
    for n in range(0, LIST, PAIR):
        weights = []
        for m in range(n, n + PAIR):
            raw = jnp.exp2((scores[m] - row_high) * LOG2_SCALE)
            total = raw if total is None else total + raw
            weights.append(raw.astype(jnp.bfloat16))
        values = jnp.concatenate(
            [kv[at[m][0], 1, pl.ds(2 * at[m][1], 2)].reshape(TILE, HD) for m in range(n, n + PAIR)], axis=0
        )
        mixed = jnp.dot(
            jnp.concatenate(weights, axis=1), values, preferred_element_type=jnp.float32
        )
        acc = mixed if acc is None else acc + mixed
    summed = jnp.sum(total, axis=1, keepdims=True)
    out_ref[out_index] = (acc / summed).astype(jnp.bfloat16).reshape(2, HALF, HD)


def attend_part(kv, q_tile, out_ref, stats, u, lists, row, length, mine, scores):
    lane = lax.broadcasted_iota(jnp.int32, (TILE, HD), 1)
    at = []
    bias = []
    for n in range(LIST):
        entry = lists[n, row]
        z = ((entry >> 5) << 1) + ((entry >> 1) & 1)
        at.append((((entry >> 2) & 1) * NZ + z) * NX + ((entry >> 3) & 3))
        bias.append(jnp.where((n < length) & ((entry & 1) == mine), 0.0, -1e30))
    high = None
    for n in range(0, LIST, 2 * PAIR):
        keys = jnp.concatenate([kv[at[m], 0] for m in range(n, n + 2 * PAIR)], axis=0)
        both = lax.dot_general(
            q_tile, keys, (((1,), (1,)), ((), ())), preferred_element_type=jnp.float32
        )
        for m in range(n, n + 2 * PAIR, 2):
            s = both[:, (m - n) * HALF:(m - n + 2) * HALF]
            s = s + jnp.where(lane[:1] < HALF, bias[m], bias[m + 1])
            scores[m // 2] = s
            high = s if high is None else jnp.maximum(high, s)
    row_high = jnp.max(high, axis=1, keepdims=True)
    total = None
    acc = None
    for n in range(0, LIST, 2 * PAIR):
        weights = []
        for m in range(n, n + 2 * PAIR, 2):
            raw = jnp.exp2((scores[m // 2] - row_high) * LOG2_SCALE)
            total = raw if total is None else total + raw
            weights.append(raw.astype(jnp.bfloat16))
        values = jnp.concatenate([kv[at[m], 1] for m in range(n, n + 2 * PAIR)], axis=0)
        mixed = jnp.dot(
            jnp.concatenate(weights, axis=1), values, preferred_element_type=jnp.float32
        )
        acc = mixed if acc is None else acc + mixed
    summed = jnp.sum(total, axis=1, keepdims=True)
    out_ref[u] = (acc / summed).astype(jnp.bfloat16)
    log_sum = row_high * LOG2_SCALE + jnp.log(summed) * math.log2(math.e)
    stats[...] = jnp.where(lane == u, log_sum, stats[...])


def fused_kernel(
    q_hbm, k_hbm, v_hbm, qg_hbm, kg_hbm, lists_hbm, lengths_hbm, out_ref,
    q_ref, k_ref, v_ref, qg_ref, kg_ref, lists, lengths,
    pack_kv, pack_q, row_kv, all_kv, queries, queries4, scores, results, parts_out, parts, stats, all_stats,
    load_sem, z_send, x_send, mate_send, q_send, out_send, part_send,
    zr_recv, z4_recv, xr_recv, x4_recv, mate_recv, q_recv, q4_recv, part_recv, out_recv,
):
    loads = []
    for n, (src, dst) in enumerate((
        (k_hbm, k_ref), (kg_hbm, kg_ref), (v_hbm, v_ref), (q_hbm, q_ref), (qg_hbm, qg_ref),
        (lists_hbm, lists), (lengths_hbm, lengths),
    )):
        copy = pltpu.make_async_copy(src, dst, load_sem.at[n])
        copy.start()
        loads.append(copy)
    x, y, z, c = place()
    barrier = pltpu.get_barrier_semaphore()
    partners = []
    for dz in range(NZ):
        for dy in range(NY):
            if dz or dy:
                partners.append(device(x, lax.rem(y + dy, NY), lax.rem(z + dz, NZ), c))
    right = device(lax.rem(x + 1, NX), y, z, c)
    left = device(lax.rem(x + NX - 1, NX), y, z, c)
    mate = device(x, y, z, 1 - c)
    partners += [right, left, mate]
    for target in partners:
        pl.semaphore_signal(barrier, inc=1, device_id=target, device_id_type=MESH)

    def put_k(h, span, part):
        pack_kv[h, 0, span, :] = part

    def put_q(h, span, part):
        pack_q[h, span, :] = part

    loads[0].wait()
    loads[1].wait()
    normalize_into(k_ref, kg_ref, put_k)
    loads[2].wait()
    for h in range(HEADS):
        pack_kv[h, 1] = v_ref[:, h * HD:(h + 1) * HD]

    pl.semaphore_wait(barrier, len(partners))

    block = (c * NZ + z) * NX + x
    for i, dz in enumerate(OFFSETS):
        zd = lax.rem(z + dz, NZ)
        src = pack_kv.at[SLICE * zd + NY]
        dst = all_kv.at[block]
        if dz:
            send(src, dst, z_send.at[0], z4_recv.at[i], device(x, y, zd, c))
        else:
            pltpu.make_async_copy(src, dst, z4_recv.at[i]).start()
    for i, dz in enumerate(OFFSETS):
        zd = lax.rem(z + dz, NZ)
        for dy in range(NY):
            yd = lax.rem(y + dy, NY)
            src = pack_kv.at[SLICE * zd + yd]
            dst = row_kv.at[block, :, y]
            if dz or dy:
                send(src, dst, z_send.at[0], zr_recv.at[i], device(x, yd, zd, c))
            else:
                pltpu.make_async_copy(src, dst, zr_recv.at[i]).start()

    loads[3].wait()
    loads[4].wait()
    normalize_into(q_ref, qg_ref, put_q)
    for dz in OFFSETS:
        zd = lax.rem(z + dz, NZ)
        src = pack_q.at[SLICE * zd + NY]
        dst = queries4.at[z, y]
        if dz:
            send(src, dst, q_send.at[0], q4_recv.at[0], device(x, y, zd, c))
        else:
            pltpu.make_async_copy(src, dst, q4_recv.at[0]).start()
    for dz in OFFSETS:
        zd = lax.rem(z + dz, NZ)
        for dy in range(NY):
            yd = lax.rem(y + dy, NY)
            src = pack_q.at[SLICE * zd + yd]
            dst = queries.at[z * NY + y]
            if dz or dy:
                send(src, dst, q_send.at[0], q_recv.at[0], device(x, yd, zd, c))
            else:
                pltpu.make_async_copy(src, dst, q_recv.at[0]).start()

    x_left, x_right, x_far = lax.rem(x + NX - 1, NX), lax.rem(x + 1, NX), lax.rem(x + 2, NX)

    def first(i):
        return (c * NZ + lax.rem(z + NZ - OFFSETS[i], NZ)) * NX

    def own_along_x(i):
        mine = row_kv.at[first(i) + x]
        await_bytes(mine, zr_recv.at[i])
        send(mine, mine, x_send.at[0], xr_recv.at[0, i], right)
        send(mine, mine, x_send.at[0], xr_recv.at[1, i], left)

    def far_along_x(i):
        from_left = row_kv.at[first(i) + x_left]
        from_right = row_kv.at[first(i) + x_right]
        await_bytes(from_left, xr_recv.at[0, i])
        await_bytes(from_right, xr_recv.at[1, i])
        from_left = row_kv.at[first(i) + x_left, 0]
        from_right = row_kv.at[first(i) + x_right, 1]
        send(from_left, from_left, x_send.at[0], xr_recv.at[2, i], right)
        send(from_right, from_right, x_send.at[0], xr_recv.at[2, i], left)

    def to_mate(i):
        await_bytes(row_kv.at[first(i) + x_far], xr_recv.at[2, i])
        whole = row_kv.at[pl.ds(first(i), NX)]
        send(whole, whole, mate_send.at[0], mate_recv.at[0], mate)

    def own_along_x4(i):
        mine = all_kv.at[first(i) + x]
        await_bytes(mine, z4_recv.at[i])
        send(mine, mine, x_send.at[1], x4_recv.at[0, i], right)
        send(mine, mine, x_send.at[1], x4_recv.at[1, i], left)

    def far_along_x4(i):
        from_left = all_kv.at[first(i) + x_left]
        from_right = all_kv.at[first(i) + x_right]
        await_bytes(from_left, x4_recv.at[0, i])
        await_bytes(from_right, x4_recv.at[1, i])
        from_left = all_kv.at[first(i) + x_left, 0]
        from_right = all_kv.at[first(i) + x_right, 1]
        send(from_left, from_left, x_send.at[1], x4_recv.at[2, i], right)
        send(from_right, from_right, x_send.at[1], x4_recv.at[2, i], left)

    def to_mate4(i):
        await_bytes(all_kv.at[first(i) + x_far], x4_recv.at[2, i])
        whole = all_kv.at[pl.ds(first(i), NX)]
        send(whole, whole, mate_send.at[1], mate_recv.at[1], mate)

    def spread_queries4():
        mine = queries4.at[:, y]
        await_bytes(mine, q4_recv.at[0])
        for dy in range(1, NY):
            target = device(x, lax.rem(y + dy, NY), z, c)
            send(mine, mine, q_send.at[1], q4_recv.at[dy], target)

    def gather_fifth():
        loads[5].wait()
        loads[6].wait()
        for dy in range(1, NY):
            await_bytes(queries4.at[:, lax.rem(y + NY - dy, NY)], q4_recv.at[dy])
        await_bytes(all_kv.at[pl.ds((1 - c) * NZ * NX, NZ * NX)], mate_recv.at[1])

    def part_unit(n, _):
        group = lax.rem(y + 1 + lax.div(n, NY), NY)
        v = lax.rem(n, NY)
        u = group * NY + v
        row = ((group * NX + x) * 2 + c) * 4 + v
        q_tile = queries4[lax.div(u, 2), pl.ds(2 * lax.rem(u, 2), 2)].reshape(TILE, HD)
        attend_part(all_kv, q_tile, parts_out, stats, u, lists, row, lengths[row], lax.div(y, 2), scores)
        src = parts_out.at[u]
        dst = parts.at[y, v]

        @pl.when(group == y)
        def _():
            pltpu.make_async_copy(src, dst, part_recv.at[0]).start()

        @pl.when(group != y)
        def _():
            send(src, dst, part_send.at[0], part_recv.at[0], device(x, group, z, c))
        return 0

    row_stages = ((5, to_mate), (3, far_along_x), (0, own_along_x))
    all_stages = ((4, to_mate4), (2, far_along_x4), (0, own_along_x4))

    def run(stages, step):
        for lag, stage in stages:
            if 0 <= step - lag < NZ:
                stage(step - lag)

    stats[...] = jnp.zeros_like(stats)
    done = 0
    for step in range(NZ + ROW_DELAY + 5):
        run(all_stages, step)
        run(row_stages, step - ROW_DELAY)
        if step == NZ:
            spread_queries4()
        count = PART_UNITS.get(step, 0)
        if count:
            if not done:
                gather_fifth()
            lax.fori_loop(done, done + count, part_unit, 0)
            done += count
    assert done == NZ * 2
    for dy in range(NY):
        dst = all_stats.at[y]
        if dy:
            target = device(x, lax.rem(y + dy, NY), z, c)
            send(stats, dst, part_send.at[1], part_recv.at[1], target)
        else:
            pltpu.make_async_copy(stats, dst, part_recv.at[1]).start()

    await_bytes(queries, q_recv.at[0])
    await_bytes(row_kv.at[pl.ds((1 - c) * NZ * NX, NZ * NX)], mate_recv.at[0])

    columns = out_ref.at[:, pl.ds(pl.multiple_of((SLICE * z + y) * HD, HD), HD)]
    columns4 = out_ref.at[:, pl.ds(pl.multiple_of((SLICE * z + NY) * HD, HD), HD)]

    def combine():
        await_bytes(parts, part_recv.at[0])
        await_bytes(all_stats, part_recv.at[1])
        lane = lax.broadcasted_iota(jnp.int32, (TILE, HD), 1)
        for v in range(NY):
            sums = [
                jnp.sum(jnp.where(lane == y * NY + v, all_stats[k], 0.0), axis=1, keepdims=True)
                for k in range(NY)
            ]
            top = jnp.maximum(jnp.maximum(sums[0], sums[1]), jnp.maximum(sums[2], sums[3]))
            shares = [jnp.exp2(part - top) for part in sums]
            whole = shares[0] + shares[1] + shares[2] + shares[3]
            mixed = shares[0] * parts[0, v].astype(jnp.float32)
            for k in range(1, NY):
                mixed = mixed + shares[k] * parts[k, v].astype(jnp.float32)
            results[NZ * 2 + v] = (mixed / whole).astype(jnp.bfloat16).reshape(2, HALF, HD)
            zd = 2 * y + v // 2
            for half in range(2):
                yd = 2 * (v % 2) + half
                src = results.at[NZ * 2 + v, half]

                @pl.when((zd == z) & (yd == y))
                def _(src=src):
                    pltpu.make_async_copy(src, columns4, out_recv.at[0]).start()

                @pl.when((zd != z) | (yd != y))
                def _(src=src, yd=yd, zd=zd):
                    send(src, columns4, out_send.at[1], out_recv.at[0], device(x, yd, zd, c))

    def row_unit(u, _):
        @pl.when(u == COMBINE_AT)
        def _():
            combine()

        k, a = lax.div(u, 2), lax.rem(u, 2)
        odd = lax.rem(k, 2)
        zd = lax.rem(z + NY + lax.div(k + odd, 2) * (2 * odd - 1), NZ)
        row = ((lax.div(zd, 2) * NX + x) * 2 + c) * 4 + lax.rem(zd, 2) * 2 + a
        mine = zd * 2 + a
        q_tile = queries[pl.ds(2 * mine, 2)].reshape(TILE, HD)
        attend_unit(row_kv, q_tile, results, mine, lists, row, lengths[row], scores)
        for half in range(2):
            yd = 2 * a + half
            src = results.at[mine, half]

            @pl.when((zd == z) & (yd == y))
            def _(src=src):
                pltpu.make_async_copy(src, columns, out_recv.at[0]).start()

            @pl.when((zd != z) | (yd != y))
            def _(src=src, yd=yd):
                send(src, columns, out_send.at[0], out_recv.at[0], device(x, yd, zd, c))
        return 0

    lax.fori_loop(0, NZ * 2, row_unit, 0)
    await_bytes(pack_kv.at[pl.ds(0, NZ * NY - 1 + NZ - 1)], z_send.at[0])
    await_bytes(pack_q.at[pl.ds(0, NZ * NY - 1 + NZ - 1)], q_send.at[0])

    @pl.when(lax.div(z, 2) != y)
    def _():
        await_bytes(pack_q.at[pl.ds(0, 2 * NY)], out_send.at[1])

    @pl.when(lax.div(z, 2) == y)
    def _():
        await_bytes(pack_q.at[pl.ds(0, 2 * NY - 1)], out_send.at[1])

    await_bytes(pack_q.at[pl.ds(0, (NY - 1) * NZ)], q_send.at[1])
    await_bytes(parts_out.at[pl.ds(0, (NY - 1) * NY)], part_send.at[0])
    await_bytes(all_stats.at[pl.ds(0, NY - 1)], part_send.at[1])
    await_bytes(row_kv.at[pl.ds(0, 3 * NZ)], x_send.at[0])
    await_bytes(all_kv.at[pl.ds(0, 3 * NZ)], x_send.at[1])
    await_bytes(row_kv.at[pl.ds(0, NX * NZ)], mate_send.at[0])
    await_bytes(all_kv.at[pl.ds(0, NX * NZ)], mate_send.at[1])
    await_bytes(pack_q.at[pl.ds(0, NZ * NY - 1)], out_send.at[0])
    await_bytes(out_ref, out_recv.at[0])


def local(query, key_in, value, query_gain, key_gain, tile_lists, list_lengths):
    rows, width = query.shape
    listed = tile_lists.T
    bf16 = jnp.bfloat16
    hbm = pl.BlockSpec(memory_space=pl.ANY)
    dma = pltpu.SemaphoreType.DMA
    return pl.pallas_call(
        fused_kernel,
        out_shape=jax.ShapeDtypeStruct((rows, width), bf16),
        in_specs=[hbm] * 7,
        out_specs=hbm,
        scratch_shapes=[
            pltpu.VMEM((rows, width), bf16),
            pltpu.VMEM((rows, width), bf16),
            pltpu.VMEM((rows, width), bf16),
            pltpu.VMEM((1, width), jnp.float32),
            pltpu.VMEM((1, width), jnp.float32),
            pltpu.SMEM(listed.shape, jnp.int32),
            pltpu.SMEM(list_lengths.shape, jnp.int32),
            pltpu.VMEM((HEADS, 2, HALF, HD), bf16),
            pltpu.VMEM((HEADS, HALF, HD), bf16),
            pltpu.VMEM((BLOCKS, 2, NY, HALF, HD), bf16),
            pltpu.VMEM((BLOCKS, 2, HALF, HD), bf16),
            pltpu.VMEM((NZ * NY, HALF, HD), bf16),
            pltpu.VMEM((NZ, NY, HALF, HD), bf16),
            pltpu.VMEM((LIST, TILE, TILE), jnp.float32),
            pltpu.VMEM((UNITS, 2, HALF, HD), bf16),
            pltpu.VMEM((NZ * 2, TILE, HD), bf16),
            pltpu.VMEM((NY, NY, TILE, HD), bf16),
            pltpu.VMEM((TILE, HD), jnp.float32),
            pltpu.VMEM((NY, TILE, HD), jnp.float32),
            dma((7,)), dma((1,)), dma((2,)), dma((2,)), dma((2,)), dma((2,)), dma((2,)),
            dma((NZ,)), dma((NZ,)), dma((3, NZ)), dma((3, NZ)), dma((2,)), dma((1,)), dma((NY,)), dma((2,)), dma((1,)),
        ],
        compiler_params=pltpu.CompilerParams(
            collective_id=0, has_side_effects=True, vmem_limit_bytes=56 * 2**20
        ),
        name="fused",
    )(
        query, key_in, value, query_gain.reshape(1, -1), key_gain.reshape(1, -1),
        listed, list_lengths,
    )


def solution(mesh):
    in_specs = (
        P(("seq", "head"), None),
        P(("seq", "head"), None),
        P(("seq", "head"), None),
        P(),
        P(),
        P(),
        P(),
    )
    out_specs = P(("seq", "head"), None)
    return jax.shard_map(local, mesh=mesh, in_specs=in_specs, out_specs=out_specs, check_vma=False)
```

```python
import math

import jax
import jax.numpy as jnp
from jax import lax
from jax.experimental import pallas as pl
from jax.experimental.pallas import tpu as pltpu
from jax.sharding import PartitionSpec as P

HD = 128
TILE = 128
HALF = 64
HEADS = 40
NX, NY, NZ, NC = 4, 4, 8, 2
SLICE = HEADS // NZ
LIST = 20
SURE = 12
PAIR = 2
LOG2_SCALE = HD ** (-0.5) * math.log2(math.e)
UNITS = 20
BLOCKS = NC * NZ * NX
MESH = pl.DeviceIdType.MESH
COMBINE_AT = 15
ROW_DELAY = 2
PART_UNITS = {11: 3, 12: 3, 13: 3, 14: 3, 15: 2, 16: 2}
QUERY_STEPS = (5, 5, 6, 6, 7, 7, 8, 8)
KV_STEPS = (-1, -1, -1, -1, -1, -1, -1, -1)
OFFSETS = (0, 1, 7, 2, 6, 3, 5, 4)


def place():
    seq = lax.axis_index("seq")
    head = lax.axis_index("head")
    c = lax.rem(seq, 2)
    x = lax.rem(lax.div(seq, 2), NX)
    z_hi = lax.div(seq, 2 * NX)
    z_lo = lax.div(head, NY)
    y = lax.rem(head, NY)
    return x, y, 2 * z_hi + z_lo, c


def device(x, y, z, c):
    return ((lax.div(z, 2) * NX + x) * 2 + c, lax.rem(z, 2) * NY + y)


def send(src, dst, send_sem, recv_sem, target):
    pltpu.make_async_remote_copy(
        src_ref=src,
        dst_ref=dst,
        send_sem=send_sem,
        recv_sem=recv_sem,
        device_id=target,
        device_id_type=MESH,
    ).start()


def await_bytes(ref, sem):
    pltpu.make_async_copy(ref, ref, sem).wait()


def normalize_into(src, gain, dst_of_head):
    def rows(block, _):
        span = pl.ds(pl.multiple_of(block * 16, 16), 16)
        squares = jnp.zeros((16, HD), jnp.float32)
        for h in range(HEADS):
            part = src[span, h * HD:(h + 1) * HD].astype(jnp.float32)
            squares = squares + part * part
        square_mean = jnp.sum(squares, axis=1, keepdims=True) * (1.0 / (HEADS * HD))
        scale = lax.rsqrt(square_mean + 1e-06)
        for h in range(HEADS):
            cols = slice(h * HD, (h + 1) * HD)
            part = src[span, cols].astype(jnp.float32) * scale * gain[:, cols]
            dst_of_head(h, span, part.astype(jnp.bfloat16))
        return 0

    lax.fori_loop(0, HALF // 16, rows, 0)


def attend_unit(kv, q_tile, out_ref, out_index, lists, row, length, scores):
    at = []
    for n in range(LIST):
        entry = lists[n, row]
        z = ((entry >> 5) << 1) + ((entry >> 1) & 1)
        at.append(((((entry >> 2) & 1) * NZ + z) * NX + ((entry >> 3) & 3), entry & 1))
    high = None
    for n in range(0, LIST, PAIR):
        keys = jnp.concatenate(
            [kv[at[m][0], 0, pl.ds(2 * at[m][1], 2)].reshape(TILE, HD) for m in range(n, n + PAIR)], axis=0
        )
        both = lax.dot_general(
            q_tile, keys, (((1,), (1,)), ((), ())), preferred_element_type=jnp.float32
        )
        for m in range(n, n + PAIR):
            s = both[:, (m - n) * TILE:(m - n + 1) * TILE]
            if m >= SURE:
                s = jnp.where(m < length, s, -1e30)
            scores[m] = s
            high = s if high is None else jnp.maximum(high, s)
    row_high = jnp.max(high, axis=1, keepdims=True)
    total = None
    acc = None
    for n in range(0, LIST, PAIR):
        weights = []
        for m in range(n, n + PAIR):
            raw = jnp.exp2((scores[m] - row_high) * LOG2_SCALE)
            total = raw if total is None else total + raw
            weights.append(raw.astype(jnp.bfloat16))
        values = jnp.concatenate(
            [kv[at[m][0], 1, pl.ds(2 * at[m][1], 2)].reshape(TILE, HD) for m in range(n, n + PAIR)], axis=0
        )
        mixed = jnp.dot(
            jnp.concatenate(weights, axis=1), values, preferred_element_type=jnp.float32
        )
        acc = mixed if acc is None else acc + mixed
    summed = jnp.sum(total, axis=1, keepdims=True)
    out_ref[out_index] = (acc / summed).astype(jnp.bfloat16).reshape(2, HALF, HD)


def attend_part(kv, q_tile, out_ref, stats, u, lists, row, length, mine, scores):
    lane = lax.broadcasted_iota(jnp.int32, (TILE, HD), 1)
    at = []
    bias = []
    for n in range(LIST):
        entry = lists[n, row]
        z = ((entry >> 5) << 1) + ((entry >> 1) & 1)
        at.append((((entry >> 2) & 1) * NZ + z) * NX + ((entry >> 3) & 3))
        bias.append(jnp.where((n < length) & ((entry & 1) == mine), 0.0, -1e30))
    high = None
    for n in range(0, LIST, 2 * PAIR):
        keys = jnp.concatenate([kv[at[m], 0] for m in range(n, n + 2 * PAIR)], axis=0)
        both = lax.dot_general(
            q_tile, keys, (((1,), (1,)), ((), ())), preferred_element_type=jnp.float32
        )
        for m in range(n, n + 2 * PAIR, 2):
            s = both[:, (m - n) * HALF:(m - n + 2) * HALF]
            s = s + jnp.where(lane[:1] < HALF, bias[m], bias[m + 1])
            scores[m // 2] = s
            high = s if high is None else jnp.maximum(high, s)
    row_high = jnp.max(high, axis=1, keepdims=True)
    total = None
    acc = None
    for n in range(0, LIST, 2 * PAIR):
        weights = []
        for m in range(n, n + 2 * PAIR, 2):
            raw = jnp.exp2((scores[m // 2] - row_high) * LOG2_SCALE)
            total = raw if total is None else total + raw
            weights.append(raw.astype(jnp.bfloat16))
        values = jnp.concatenate([kv[at[m], 1] for m in range(n, n + 2 * PAIR)], axis=0)
        mixed = jnp.dot(
            jnp.concatenate(weights, axis=1), values, preferred_element_type=jnp.float32
        )
        acc = mixed if acc is None else acc + mixed
    summed = jnp.sum(total, axis=1, keepdims=True)
    out_ref[u] = (acc / summed).astype(jnp.bfloat16)
    log_sum = row_high * LOG2_SCALE + jnp.log(summed) * math.log2(math.e)
    stats[...] = jnp.where(lane == u, log_sum, stats[...])


def fused_kernel(
    q_hbm, k_hbm, v_hbm, qg_hbm, kg_hbm, lists_hbm, lengths_hbm, out_ref,
    q_ref, k_ref, v_ref, qg_ref, kg_ref, lists, lengths,
    pack_kv, pack_q, row_kv, all_kv, queries, queries4, scores, results, parts_out, parts, stats, all_stats, landing,
    load_sem, z_send, x_send, mate_send, q_send, out_send, part_send,
    zr_recv, z4_recv, xr_recv, x4_recv, mate_recv, q_recv, q4_recv, part_recv, out_recv,
):
    loads = []
    for n, (src, dst) in enumerate((
        (k_hbm, k_ref), (kg_hbm, kg_ref), (v_hbm, v_ref), (q_hbm, q_ref), (qg_hbm, qg_ref),
        (lists_hbm, lists), (lengths_hbm, lengths),
    )):
        copy = pltpu.make_async_copy(src, dst, load_sem.at[n])
        copy.start()
        loads.append(copy)
    x, y, z, c = place()
    barrier = pltpu.get_barrier_semaphore()
    partners = []
    for dz in range(NZ):
        for dy in range(NY):
            if dz or dy:
                partners.append(device(x, lax.rem(y + dy, NY), lax.rem(z + dz, NZ), c))
    right = device(lax.rem(x + 1, NX), y, z, c)
    left = device(lax.rem(x + NX - 1, NX), y, z, c)
    mate = device(x, y, z, 1 - c)
    partners += [right, left, mate]
    for target in partners:
        pl.semaphore_signal(barrier, inc=1, device_id=target, device_id_type=MESH)

    def put_k(h, span, part):
        pack_kv[h, 0, span, :] = part

    def put_q(h, span, part):
        pack_q[h, span, :] = part

    loads[0].wait()
    loads[1].wait()
    normalize_into(k_ref, kg_ref, put_k)
    loads[2].wait()
    for h in range(HEADS):
        pack_kv[h, 1] = v_ref[:, h * HD:(h + 1) * HD]

    pl.semaphore_wait(barrier, len(partners))

    block = (c * NZ + z) * NX + x
    for i, dz in enumerate(OFFSETS):
        zd = lax.rem(z + dz, NZ)
        src = pack_kv.at[SLICE * zd + NY]
        dst = all_kv.at[block]
        if dz:
            send(src, dst, z_send.at[0], z4_recv.at[i], device(x, y, zd, c))
        else:
            pltpu.make_async_copy(src, dst, z4_recv.at[i]).start()
    def issue_row_kv(i):
        dz = OFFSETS[i]
        zd = lax.rem(z + dz, NZ)
        for dy in range(NY):
            yd = lax.rem(y + dy, NY)
            src = pack_kv.at[SLICE * zd + yd]
            dst = row_kv.at[block, :, y]
            if dz or dy:
                send(src, dst, z_send.at[0], zr_recv.at[i], device(x, yd, zd, c))
            else:
                pltpu.make_async_copy(src, dst, zr_recv.at[i]).start()

    for i in range(NZ):
        if KV_STEPS[i] < 0:
            issue_row_kv(i)

    loads[3].wait()
    loads[4].wait()
    normalize_into(q_ref, qg_ref, put_q)
    for dz in OFFSETS:
        zd = lax.rem(z + dz, NZ)
        src = pack_q.at[SLICE * zd + NY]
        dst = queries4.at[z, y]
        if dz:
            send(src, dst, q_send.at[0], q4_recv.at[0], device(x, y, zd, c))
        else:
            pltpu.make_async_copy(src, dst, q4_recv.at[0]).start()
    def issue_queries(dz):
        zd = lax.rem(z + dz, NZ)
        for dy in range(NY):
            yd = lax.rem(y + dy, NY)
            src = pack_q.at[SLICE * zd + yd]
            dst = queries.at[z * NY + y]
            if dz or dy:
                send(src, dst, q_send.at[0], q_recv.at[0], device(x, yd, zd, c))
            else:
                pltpu.make_async_copy(src, dst, q_recv.at[0]).start()

    x_left, x_right, x_far = lax.rem(x + NX - 1, NX), lax.rem(x + 1, NX), lax.rem(x + 2, NX)

    def first(i):
        return (c * NZ + lax.rem(z + NZ - OFFSETS[i], NZ)) * NX

    def own_along_x(i):
        mine = row_kv.at[first(i) + x]
        await_bytes(mine, zr_recv.at[i])
        send(mine, mine, x_send.at[0], xr_recv.at[0, i], right)
        send(mine, mine, x_send.at[0], xr_recv.at[1, i], left)

    def far_along_x(i):
        from_left = row_kv.at[first(i) + x_left]
        from_right = row_kv.at[first(i) + x_right]
        await_bytes(from_left, xr_recv.at[0, i])
        await_bytes(from_right, xr_recv.at[1, i])
        from_left = row_kv.at[first(i) + x_left, 0]
        from_right = row_kv.at[first(i) + x_right, 1]
        send(from_left, from_left, x_send.at[0], xr_recv.at[2, i], right)
        send(from_right, from_right, x_send.at[0], xr_recv.at[2, i], left)

    def to_mate(i):
        await_bytes(row_kv.at[first(i) + x_far], xr_recv.at[2, i])
        whole = row_kv.at[pl.ds(first(i), NX)]
        send(whole, whole, mate_send.at[0], mate_recv.at[0], mate)

    def own_along_x4(i):
        mine = all_kv.at[first(i) + x]
        await_bytes(mine, z4_recv.at[i])
        send(mine, mine, x_send.at[1], x4_recv.at[0, i], right)
        send(mine, mine, x_send.at[1], x4_recv.at[1, i], left)

    def far_along_x4(i):
        from_left = all_kv.at[first(i) + x_left]
        from_right = all_kv.at[first(i) + x_right]
        await_bytes(from_left, x4_recv.at[0, i])
        await_bytes(from_right, x4_recv.at[1, i])
        from_left = all_kv.at[first(i) + x_left, 0]
        from_right = all_kv.at[first(i) + x_right, 1]
        send(from_left, from_left, x_send.at[1], x4_recv.at[2, i], right)
        send(from_right, from_right, x_send.at[1], x4_recv.at[2, i], left)

    def to_mate4(i):
        await_bytes(all_kv.at[first(i) + x_far], x4_recv.at[2, i])
        whole = all_kv.at[pl.ds(first(i), NX)]
        send(whole, whole, mate_send.at[1], mate_recv.at[1], mate)

    def spread_queries4():
        mine = queries4.at[:, y]
        await_bytes(mine, q4_recv.at[0])
        for dy in range(1, NY):
            target = device(x, lax.rem(y + dy, NY), z, c)
            send(mine, mine, q_send.at[1], q4_recv.at[dy], target)

    def gather_fifth():
        loads[5].wait()
        loads[6].wait()
        for dy in range(1, NY):
            await_bytes(queries4.at[:, lax.rem(y + NY - dy, NY)], q4_recv.at[dy])
        await_bytes(all_kv.at[pl.ds((1 - c) * NZ * NX, NZ * NX)], mate_recv.at[1])

    def part_unit(n, _):
        group = lax.rem(y + 1 + lax.div(n, NY), NY)
        v = lax.rem(n, NY)
        u = group * NY + v
        row = ((group * NX + x) * 2 + c) * 4 + v
        q_tile = queries4[lax.div(u, 2), pl.ds(2 * lax.rem(u, 2), 2)].reshape(TILE, HD)
        attend_part(all_kv, q_tile, parts_out, stats, u, lists, row, lengths[row], lax.div(y, 2), scores)
        src = parts_out.at[u]
        dst = parts.at[y, v]

        @pl.when(group == y)
        def _():
            pltpu.make_async_copy(src, dst, part_recv.at[0]).start()

        @pl.when(group != y)
        def _():
            send(src, dst, part_send.at[0], part_recv.at[0], device(x, group, z, c))
        return 0

    row_stages = ((7, to_mate), (4, far_along_x), (0, own_along_x))
    all_stages = ((4, to_mate4), (2, far_along_x4), (0, own_along_x4))

    def run(stages, step):
        for lag, stage in stages:
            if 0 <= step - lag < NZ:
                stage(step - lag)

    stats[...] = jnp.zeros_like(stats)
    done = 0
    for step in range(NZ + ROW_DELAY + 7):
        run(all_stages, step)
        run(row_stages, step - ROW_DELAY)
        for i, dz in enumerate(OFFSETS):
            if QUERY_STEPS[i] == step:
                issue_queries(dz)
            if KV_STEPS[i] == step:
                issue_row_kv(i)
        if step == NZ:
            spread_queries4()
        count = PART_UNITS.get(step, 0)
        if count:
            if not done:
                gather_fifth()
            lax.fori_loop(done, done + count, part_unit, 0)
            done += count
    assert done == NZ * 2
    for dy in range(NY):
        dst = all_stats.at[y]
        if dy:
            target = device(x, lax.rem(y + dy, NY), z, c)
            send(stats, dst, part_send.at[1], part_recv.at[1], target)
        else:
            pltpu.make_async_copy(stats, dst, part_recv.at[1]).start()

    await_bytes(queries, q_recv.at[0])
    await_bytes(row_kv.at[pl.ds((1 - c) * NZ * NX, NZ * NX)], mate_recv.at[0])

    columns = landing.at[SLICE * z + y]
    columns4 = landing.at[SLICE * z + NY]

    def combine():
        await_bytes(parts, part_recv.at[0])
        await_bytes(all_stats, part_recv.at[1])
        lane = lax.broadcasted_iota(jnp.int32, (TILE, HD), 1)
        for v in range(NY):
            sums = [
                jnp.sum(jnp.where(lane == y * NY + v, all_stats[k], 0.0), axis=1, keepdims=True)
                for k in range(NY)
            ]
            top = jnp.maximum(jnp.maximum(sums[0], sums[1]), jnp.maximum(sums[2], sums[3]))
            shares = [jnp.exp2(part - top) for part in sums]
            whole = shares[0] + shares[1] + shares[2] + shares[3]
            mixed = shares[0] * parts[0, v].astype(jnp.float32)
            for k in range(1, NY):
                mixed = mixed + shares[k] * parts[k, v].astype(jnp.float32)
            results[NZ * 2 + v] = (mixed / whole).astype(jnp.bfloat16).reshape(2, HALF, HD)
            zd = 2 * y + v // 2
            for half in range(2):
                yd = 2 * (v % 2) + half
                src = results.at[NZ * 2 + v, half]

                @pl.when((zd == z) & (yd == y))
                def _(src=src):
                    pltpu.make_async_copy(src, columns4, out_recv.at[0]).start()

                @pl.when((zd != z) | (yd != y))
                def _(src=src, yd=yd, zd=zd):
                    send(src, columns4, out_send.at[1], out_recv.at[0], device(x, yd, zd, c))

    def row_unit(u, _):
        @pl.when(u == COMBINE_AT)
        def _():
            combine()

        k, a = lax.div(u, 2), lax.rem(u, 2)
        odd = lax.rem(k, 2)
        zd = lax.rem(z + NY + lax.div(k + odd, 2) * (2 * odd - 1), NZ)
        row = ((lax.div(zd, 2) * NX + x) * 2 + c) * 4 + lax.rem(zd, 2) * 2 + a
        mine = zd * 2 + a
        q_tile = queries[pl.ds(2 * mine, 2)].reshape(TILE, HD)
        attend_unit(row_kv, q_tile, results, mine, lists, row, lengths[row], scores)
        for half in range(2):
            yd = 2 * a + half
            src = results.at[mine, half]

            @pl.when((zd == z) & (yd == y))
            def _(src=src):
                pltpu.make_async_copy(src, columns, out_recv.at[0]).start()

            @pl.when((zd != z) | (yd != y))
            def _(src=src, yd=yd):
                send(src, columns, out_send.at[0], out_recv.at[0], device(x, yd, zd, c))
        return 0

    lax.fori_loop(0, NZ * 2, row_unit, 0)
    await_bytes(pack_kv.at[pl.ds(0, NZ * NY - 1 + NZ - 1)], z_send.at[0])
    await_bytes(pack_q.at[pl.ds(0, NZ * NY - 1 + NZ - 1)], q_send.at[0])

    @pl.when(lax.div(z, 2) != y)
    def _():
        await_bytes(pack_q.at[pl.ds(0, 2 * NY)], out_send.at[1])

    @pl.when(lax.div(z, 2) == y)
    def _():
        await_bytes(pack_q.at[pl.ds(0, 2 * NY - 1)], out_send.at[1])

    await_bytes(pack_q.at[pl.ds(0, (NY - 1) * NZ)], q_send.at[1])
    await_bytes(parts_out.at[pl.ds(0, (NY - 1) * NY)], part_send.at[0])
    await_bytes(all_stats.at[pl.ds(0, NY - 1)], part_send.at[1])
    await_bytes(row_kv.at[pl.ds(0, 3 * NZ)], x_send.at[0])
    await_bytes(all_kv.at[pl.ds(0, 3 * NZ)], x_send.at[1])
    await_bytes(row_kv.at[pl.ds(0, NX * NZ)], mate_send.at[0])
    await_bytes(all_kv.at[pl.ds(0, NX * NZ)], mate_send.at[1])
    await_bytes(pack_q.at[pl.ds(0, NZ * NY - 1)], out_send.at[0])
    await_bytes(landing, out_recv.at[0])
    for h in range(HEADS):
        out_ref[:, h * HD:(h + 1) * HD] = landing[h]


def local(query, key_in, value, query_gain, key_gain, tile_lists, list_lengths):
    rows, width = query.shape
    listed = tile_lists.T
    bf16 = jnp.bfloat16
    hbm = pl.BlockSpec(memory_space=pl.ANY)
    dma = pltpu.SemaphoreType.DMA
    return pl.pallas_call(
        fused_kernel,
        out_shape=jax.ShapeDtypeStruct((rows, width), bf16),
        in_specs=[hbm] * 7,
        out_specs=pl.BlockSpec(memory_space=pltpu.VMEM),
        scratch_shapes=[
            pltpu.VMEM((rows, width), bf16),
            pltpu.VMEM((rows, width), bf16),
            pltpu.VMEM((rows, width), bf16),
            pltpu.VMEM((1, width), jnp.float32),
            pltpu.VMEM((1, width), jnp.float32),
            pltpu.SMEM(listed.shape, jnp.int32),
            pltpu.SMEM(list_lengths.shape, jnp.int32),
            pltpu.VMEM((HEADS, 2, HALF, HD), bf16),
            pltpu.VMEM((HEADS, HALF, HD), bf16),
            pltpu.VMEM((BLOCKS, 2, NY, HALF, HD), bf16),
            pltpu.VMEM((BLOCKS, 2, HALF, HD), bf16),
            pltpu.VMEM((NZ * NY, HALF, HD), bf16),
            pltpu.VMEM((NZ, NY, HALF, HD), bf16),
            pltpu.VMEM((LIST, TILE, TILE), jnp.float32),
            pltpu.VMEM((UNITS, 2, HALF, HD), bf16),
            pltpu.VMEM((NZ * 2, TILE, HD), bf16),
            pltpu.VMEM((NY, NY, TILE, HD), bf16),
            pltpu.VMEM((TILE, HD), jnp.float32),
            pltpu.VMEM((NY, TILE, HD), jnp.float32),
            pltpu.VMEM((HEADS, HALF, HD), bf16),
            dma((7,)), dma((1,)), dma((2,)), dma((2,)), dma((2,)), dma((2,)), dma((2,)),
            dma((NZ,)), dma((NZ,)), dma((3, NZ)), dma((3, NZ)), dma((2,)), dma((1,)), dma((NY,)), dma((2,)), dma((1,)),
        ],
        compiler_params=pltpu.CompilerParams(
            collective_id=0, has_side_effects=True, vmem_limit_bytes=56 * 2**20
        ),
        name="fused",
    )(
        query, key_in, value, query_gain.reshape(1, -1), key_gain.reshape(1, -1),
        listed, list_lengths,
    )


def solution(mesh):
    in_specs = (
        P(("seq", "head"), None),
        P(("seq", "head"), None),
        P(("seq", "head"), None),
        P(),
        P(),
        P(),
        P(),
    )
    out_specs = P(("seq", "head"), None)
    return jax.shard_map(local, mesh=mesh, in_specs=in_specs, out_specs=out_specs, check_vma=False)
```

```python
import math

import jax
import jax.numpy as jnp
from jax import lax
from jax.experimental import pallas as pl
from jax.experimental.pallas import tpu as pltpu
from jax.sharding import PartitionSpec as P

HD = 128
TILE = 128
HALF = 64
HEADS = 40
NX, NY, NZ, NC = 4, 4, 8, 2
SLICE = HEADS // NZ
LIST = 20
SURE = 12
PAIR = 2
LOG2_SCALE = HD ** (-0.5) * math.log2(math.e)
UNITS = 20
BLOCKS = NC * NZ * NX
MESH = pl.DeviceIdType.MESH
COMBINE_AT = 15
ROW_DELAY = 2
PART_UNITS = {11: 2, 12: 2, 13: 2, 14: 2, 15: 4, 16: 4}
QUERY_STEPS = (5, 5, 6, 6, 7, 7, 8, 8)
KV_STEPS = (-1, -1, -1, -1, -1, -1, -1, -1)
OFFSETS = (0, 1, 7, 2, 6, 4, 3, 5)


def place():
    seq = lax.axis_index("seq")
    head = lax.axis_index("head")
    c = lax.rem(seq, 2)
    x = lax.rem(lax.div(seq, 2), NX)
    z_hi = lax.div(seq, 2 * NX)
    z_lo = lax.div(head, NY)
    y = lax.rem(head, NY)
    return x, y, 2 * z_hi + z_lo, c


def device(x, y, z, c):
    return ((lax.div(z, 2) * NX + x) * 2 + c, lax.rem(z, 2) * NY + y)


def send(src, dst, send_sem, recv_sem, target):
    pltpu.make_async_remote_copy(
        src_ref=src,
        dst_ref=dst,
        send_sem=send_sem,
        recv_sem=recv_sem,
        device_id=target,
        device_id_type=MESH,
    ).start()


def await_bytes(ref, sem):
    pltpu.make_async_copy(ref, ref, sem).wait()


def normalize_into(src, gain, dst_of_head):
    def rows(block, _):
        span = pl.ds(pl.multiple_of(block * 16, 16), 16)
        squares = jnp.zeros((16, HD), jnp.float32)
        for h in range(HEADS):
            part = src[span, h * HD:(h + 1) * HD].astype(jnp.float32)
            squares = squares + part * part
        square_mean = jnp.sum(squares, axis=1, keepdims=True) * (1.0 / (HEADS * HD))
        scale = lax.rsqrt(square_mean + 1e-06)
        for h in range(HEADS):
            cols = slice(h * HD, (h + 1) * HD)
            part = src[span, cols].astype(jnp.float32) * scale * gain[:, cols]
            dst_of_head(h, span, part.astype(jnp.bfloat16))
        return 0

    lax.fori_loop(0, HALF // 16, rows, 0)


def attend_unit(kv, q_tile, out_ref, out_index, lists, row, length, scores):
    at = []
    for n in range(LIST):
        entry = lists[n, row]
        z = ((entry >> 5) << 1) + ((entry >> 1) & 1)
        at.append(((((entry >> 2) & 1) * NZ + z) * NX + ((entry >> 3) & 3), entry & 1))
    high = None
    for n in range(0, LIST, PAIR):
        keys = jnp.concatenate(
            [kv[at[m][0], 0, pl.ds(2 * at[m][1], 2)].reshape(TILE, HD) for m in range(n, n + PAIR)], axis=0
        )
        both = lax.dot_general(
            q_tile, keys, (((1,), (1,)), ((), ())), preferred_element_type=jnp.float32
        )
        for m in range(n, n + PAIR):
            s = both[:, (m - n) * TILE:(m - n + 1) * TILE]
            if m >= SURE:
                s = jnp.where(m < length, s, -1e30)
            scores[m] = s
            high = s if high is None else jnp.maximum(high, s)
    row_high = jnp.max(high, axis=1, keepdims=True)
    total = None
    acc = None
    for n in range(0, LIST, PAIR):
        weights = []
        for m in range(n, n + PAIR):
            raw = jnp.exp2((scores[m] - row_high) * LOG2_SCALE)
            total = raw if total is None else total + raw
            weights.append(raw.astype(jnp.bfloat16))
        values = jnp.concatenate(
            [kv[at[m][0], 1, pl.ds(2 * at[m][1], 2)].reshape(TILE, HD) for m in range(n, n + PAIR)], axis=0
        )
        mixed = jnp.dot(
            jnp.concatenate(weights, axis=1), values, preferred_element_type=jnp.float32
        )
        acc = mixed if acc is None else acc + mixed
    summed = jnp.sum(total, axis=1, keepdims=True)
    out_ref[out_index] = (acc / summed).astype(jnp.bfloat16).reshape(2, HALF, HD)


def attend_part(kv, q_tile, out_ref, stats, u, lists, row, length, mine, scores):
    lane = lax.broadcasted_iota(jnp.int32, (TILE, HD), 1)
    at = []
    bias = []
    for n in range(LIST):
        entry = lists[n, row]
        z = ((entry >> 5) << 1) + ((entry >> 1) & 1)
        at.append((((entry >> 2) & 1) * NZ + z) * NX + ((entry >> 3) & 3))
        bias.append(jnp.where((n < length) & ((entry & 1) == mine), 0.0, -1e30))
    high = None
    for n in range(0, LIST, 2 * PAIR):
        keys = jnp.concatenate([kv[at[m], 0] for m in range(n, n + 2 * PAIR)], axis=0)
        both = lax.dot_general(
            q_tile, keys, (((1,), (1,)), ((), ())), preferred_element_type=jnp.float32
        )
        for m in range(n, n + 2 * PAIR, 2):
            s = both[:, (m - n) * HALF:(m - n + 2) * HALF]
            s = s + jnp.where(lane[:1] < HALF, bias[m], bias[m + 1])
            scores[m // 2] = s
            high = s if high is None else jnp.maximum(high, s)
    row_high = jnp.max(high, axis=1, keepdims=True)
    total = None
    acc = None
    for n in range(0, LIST, 2 * PAIR):
        weights = []
        for m in range(n, n + 2 * PAIR, 2):
            raw = jnp.exp2((scores[m // 2] - row_high) * LOG2_SCALE)
            total = raw if total is None else total + raw
            weights.append(raw.astype(jnp.bfloat16))
        values = jnp.concatenate([kv[at[m], 1] for m in range(n, n + 2 * PAIR)], axis=0)
        mixed = jnp.dot(
            jnp.concatenate(weights, axis=1), values, preferred_element_type=jnp.float32
        )
        acc = mixed if acc is None else acc + mixed
    summed = jnp.sum(total, axis=1, keepdims=True)
    out_ref[u] = (acc / summed).astype(jnp.bfloat16)
    log_sum = row_high * LOG2_SCALE + jnp.log(summed) * math.log2(math.e)
    stats[...] = jnp.where(lane == u, log_sum, stats[...])


def fused_kernel(
    q_hbm, k_hbm, v_hbm, qg_hbm, kg_hbm, lists_hbm, lengths_hbm, out_ref,
    q_ref, k_ref, v_ref, qg_ref, kg_ref, lists, lengths,
    pack_kv, pack_q, row_kv, all_kv, queries, queries4, scores, results, parts_out, parts, stats, all_stats, landing,
    load_sem, z_send, x_send, mate_send, q_send, out_send, part_send,
    zr_recv, z4_recv, xr_recv, x4_recv, mate_recv, q_recv, q4_recv, part_recv, out_recv,
):
    loads = []
    for n, (src, dst) in enumerate((
        (k_hbm, k_ref), (kg_hbm, kg_ref), (v_hbm, v_ref), (q_hbm, q_ref), (qg_hbm, qg_ref),
        (lists_hbm, lists), (lengths_hbm, lengths),
    )):
        copy = pltpu.make_async_copy(src, dst, load_sem.at[n])
        copy.start()
        loads.append(copy)
    x, y, z, c = place()
    barrier = pltpu.get_barrier_semaphore()
    partners = []
    for dz in range(NZ):
        for dy in range(NY):
            if dz or dy:
                partners.append(device(x, lax.rem(y + dy, NY), lax.rem(z + dz, NZ), c))
    right = device(lax.rem(x + 1, NX), y, z, c)
    left = device(lax.rem(x + NX - 1, NX), y, z, c)
    mate = device(x, y, z, 1 - c)
    partners += [right, left, mate]
    for target in partners:
        pl.semaphore_signal(barrier, inc=1, device_id=target, device_id_type=MESH)

    def put_k(h, span, part):
        pack_kv[h, 0, span, :] = part

    def put_q(h, span, part):
        pack_q[h, span, :] = part

    loads[0].wait()
    loads[1].wait()
    normalize_into(k_ref, kg_ref, put_k)
    loads[2].wait()
    for h in range(HEADS):
        pack_kv[h, 1] = v_ref[:, h * HD:(h + 1) * HD]

    pl.semaphore_wait(barrier, len(partners))

    block = (c * NZ + z) * NX + x
    for i, dz in enumerate(OFFSETS):
        zd = lax.rem(z + dz, NZ)
        src = pack_kv.at[SLICE * zd + NY]
        dst = all_kv.at[block]
        if dz:
            send(src, dst, z_send.at[0], z4_recv.at[i], device(x, y, zd, c))
        else:
            pltpu.make_async_copy(src, dst, z4_recv.at[i]).start()
    def issue_row_kv(i):
        dz = OFFSETS[i]
        zd = lax.rem(z + dz, NZ)
        for dy in range(NY):
            yd = lax.rem(y + dy, NY)
            src = pack_kv.at[SLICE * zd + yd]
            dst = row_kv.at[block, :, y]
            if dz or dy:
                send(src, dst, z_send.at[0], zr_recv.at[i], device(x, yd, zd, c))
            else:
                pltpu.make_async_copy(src, dst, zr_recv.at[i]).start()

    for i in range(NZ):
        if KV_STEPS[i] < 0:
            issue_row_kv(i)

    loads[3].wait()
    loads[4].wait()
    normalize_into(q_ref, qg_ref, put_q)
    for dz in OFFSETS:
        zd = lax.rem(z + dz, NZ)
        src = pack_q.at[SLICE * zd + NY]
        dst = queries4.at[z, y]
        if dz:
            send(src, dst, q_send.at[0], q4_recv.at[0], device(x, y, zd, c))
        else:
            pltpu.make_async_copy(src, dst, q4_recv.at[0]).start()
    def issue_queries(dz):
        zd = lax.rem(z + dz, NZ)
        for dy in range(NY):
            yd = lax.rem(y + dy, NY)
            src = pack_q.at[SLICE * zd + yd]
            dst = queries.at[z * NY + y]
            if dz or dy:
                send(src, dst, q_send.at[0], q_recv.at[0], device(x, yd, zd, c))
            else:
                pltpu.make_async_copy(src, dst, q_recv.at[0]).start()

    x_left, x_right, x_far = lax.rem(x + NX - 1, NX), lax.rem(x + 1, NX), lax.rem(x + 2, NX)

    def first(i):
        return (c * NZ + lax.rem(z + NZ - OFFSETS[i], NZ)) * NX

    def own_along_x(i):
        mine = row_kv.at[first(i) + x]
        await_bytes(mine, zr_recv.at[i])
        send(mine, mine, x_send.at[0], xr_recv.at[0, i], right)
        send(mine, mine, x_send.at[0], xr_recv.at[1, i], left)

    def far_along_x(i):
        from_left = row_kv.at[first(i) + x_left]
        from_right = row_kv.at[first(i) + x_right]
        await_bytes(from_left, xr_recv.at[0, i])
        await_bytes(from_right, xr_recv.at[1, i])
        from_left = row_kv.at[first(i) + x_left, 0]
        from_right = row_kv.at[first(i) + x_right, 1]
        send(from_left, from_left, x_send.at[0], xr_recv.at[2, i], right)
        send(from_right, from_right, x_send.at[0], xr_recv.at[2, i], left)

    def to_mate(i):
        await_bytes(row_kv.at[first(i) + x_far], xr_recv.at[2, i])
        whole = row_kv.at[pl.ds(first(i), NX)]
        send(whole, whole, mate_send.at[0], mate_recv.at[0], mate)

    def own_along_x4(i):
        mine = all_kv.at[first(i) + x]
        await_bytes(mine, z4_recv.at[i])
        send(mine, mine, x_send.at[1], x4_recv.at[0, i], right)
        send(mine, mine, x_send.at[1], x4_recv.at[1, i], left)

    def far_along_x4(i):
        from_left = all_kv.at[first(i) + x_left]
        from_right = all_kv.at[first(i) + x_right]
        await_bytes(from_left, x4_recv.at[0, i])
        await_bytes(from_right, x4_recv.at[1, i])
        from_left = all_kv.at[first(i) + x_left, 0]
        from_right = all_kv.at[first(i) + x_right, 1]
        send(from_left, from_left, x_send.at[1], x4_recv.at[2, i], right)
        send(from_right, from_right, x_send.at[1], x4_recv.at[2, i], left)

    def to_mate4(i):
        await_bytes(all_kv.at[first(i) + x_far], x4_recv.at[2, i])
        whole = all_kv.at[pl.ds(first(i), NX)]
        send(whole, whole, mate_send.at[1], mate_recv.at[1], mate)

    def spread_queries4():
        mine = queries4.at[:, y]
        await_bytes(mine, q4_recv.at[0])
        for dy in range(1, NY):
            target = device(x, lax.rem(y + dy, NY), z, c)
            send(mine, mine, q_send.at[1], q4_recv.at[dy], target)

    def gather_fifth():
        loads[5].wait()
        loads[6].wait()
        for dy in range(1, NY):
            await_bytes(queries4.at[:, lax.rem(y + NY - dy, NY)], q4_recv.at[dy])
        await_bytes(all_kv.at[pl.ds((1 - c) * NZ * NX, NZ * NX)], mate_recv.at[1])

    def part_unit(n, _):
        group = lax.rem(y + 1 + lax.div(n, NY), NY)
        v = lax.rem(n, NY)
        u = group * NY + v
        row = ((group * NX + x) * 2 + c) * 4 + v
        q_tile = queries4[lax.div(u, 2), pl.ds(2 * lax.rem(u, 2), 2)].reshape(TILE, HD)
        attend_part(all_kv, q_tile, parts_out, stats, u, lists, row, lengths[row], lax.div(y, 2), scores)
        src = parts_out.at[u]
        dst = parts.at[y, v]

        @pl.when(group == y)
        def _():
            pltpu.make_async_copy(src, dst, part_recv.at[0]).start()

        @pl.when(group != y)
        def _():
            send(src, dst, part_send.at[0], part_recv.at[0], device(x, group, z, c))
        return 0

    row_stages = ((7, to_mate), (4, far_along_x), (0, own_along_x))
    all_stages = ((4, to_mate4), (2, far_along_x4), (0, own_along_x4))

    def run(stages, step):
        for lag, stage in stages:
            if 0 <= step - lag < NZ:
                stage(step - lag)

    stats[...] = jnp.zeros_like(stats)
    done = 0
    for step in range(NZ + ROW_DELAY + 7):
        run(all_stages, step)
        run(row_stages, step - ROW_DELAY)
        for i, dz in enumerate(OFFSETS):
            if QUERY_STEPS[i] == step:
                issue_queries(dz)
            if KV_STEPS[i] == step:
                issue_row_kv(i)
        if step == NZ:
            spread_queries4()
        count = PART_UNITS.get(step, 0)
        if count:
            if not done:
                gather_fifth()
            lax.fori_loop(done, done + count, part_unit, 0)
            done += count
    assert done == NZ * 2
    for dy in range(NY):
        dst = all_stats.at[y]
        if dy:
            target = device(x, lax.rem(y + dy, NY), z, c)
            send(stats, dst, part_send.at[1], part_recv.at[1], target)
        else:
            pltpu.make_async_copy(stats, dst, part_recv.at[1]).start()

    await_bytes(queries, q_recv.at[0])
    await_bytes(row_kv.at[pl.ds((1 - c) * NZ * NX, NZ * NX)], mate_recv.at[0])

    columns = landing.at[SLICE * z + y]
    columns4 = landing.at[SLICE * z + NY]

    def combine():
        await_bytes(parts, part_recv.at[0])
        await_bytes(all_stats, part_recv.at[1])
        lane = lax.broadcasted_iota(jnp.int32, (TILE, HD), 1)
        for v in range(NY):
            sums = [
                jnp.sum(jnp.where(lane == y * NY + v, all_stats[k], 0.0), axis=1, keepdims=True)
                for k in range(NY)
            ]
            top = jnp.maximum(jnp.maximum(sums[0], sums[1]), jnp.maximum(sums[2], sums[3]))
            shares = [jnp.exp2(part - top) for part in sums]
            whole = shares[0] + shares[1] + shares[2] + shares[3]
            mixed = shares[0] * parts[0, v].astype(jnp.float32)
            for k in range(1, NY):
                mixed = mixed + shares[k] * parts[k, v].astype(jnp.float32)
            results[NZ * 2 + v] = (mixed / whole).astype(jnp.bfloat16).reshape(2, HALF, HD)
            zd = 2 * y + v // 2
            for half in range(2):
                yd = 2 * (v % 2) + half
                src = results.at[NZ * 2 + v, half]

                @pl.when((zd == z) & (yd == y))
                def _(src=src):
                    pltpu.make_async_copy(src, columns4, out_recv.at[0]).start()

                @pl.when((zd != z) | (yd != y))
                def _(src=src, yd=yd, zd=zd):
                    send(src, columns4, out_send.at[1], out_recv.at[0], device(x, yd, zd, c))

    def row_unit(u, _):
        @pl.when(u == COMBINE_AT)
        def _():
            combine()

        k, a = lax.div(u, 2), lax.rem(u, 2)
        odd = lax.rem(k, 2)
        zd = lax.rem(z + NY + lax.div(k + odd, 2) * (2 * odd - 1), NZ)
        row = ((lax.div(zd, 2) * NX + x) * 2 + c) * 4 + lax.rem(zd, 2) * 2 + a
        mine = zd * 2 + a
        q_tile = queries[pl.ds(2 * mine, 2)].reshape(TILE, HD)
        attend_unit(row_kv, q_tile, results, mine, lists, row, lengths[row], scores)
        for half in range(2):
            yd = 2 * a + half
            src = results.at[mine, half]

            @pl.when((zd == z) & (yd == y))
            def _(src=src):
                pltpu.make_async_copy(src, columns, out_recv.at[0]).start()

            @pl.when((zd != z) | (yd != y))
            def _(src=src, yd=yd):
                send(src, columns, out_send.at[0], out_recv.at[0], device(x, yd, zd, c))
        return 0

    lax.fori_loop(0, NZ * 2, row_unit, 0)
    await_bytes(pack_kv.at[pl.ds(0, NZ * NY - 1 + NZ - 1)], z_send.at[0])
    await_bytes(pack_q.at[pl.ds(0, NZ * NY - 1 + NZ - 1)], q_send.at[0])

    @pl.when(lax.div(z, 2) != y)
    def _():
        await_bytes(pack_q.at[pl.ds(0, 2 * NY)], out_send.at[1])

    @pl.when(lax.div(z, 2) == y)
    def _():
        await_bytes(pack_q.at[pl.ds(0, 2 * NY - 1)], out_send.at[1])

    await_bytes(pack_q.at[pl.ds(0, (NY - 1) * NZ)], q_send.at[1])
    await_bytes(parts_out.at[pl.ds(0, (NY - 1) * NY)], part_send.at[0])
    await_bytes(all_stats.at[pl.ds(0, NY - 1)], part_send.at[1])
    await_bytes(row_kv.at[pl.ds(0, 3 * NZ)], x_send.at[0])
    await_bytes(all_kv.at[pl.ds(0, 3 * NZ)], x_send.at[1])
    await_bytes(row_kv.at[pl.ds(0, NX * NZ)], mate_send.at[0])
    await_bytes(all_kv.at[pl.ds(0, NX * NZ)], mate_send.at[1])
    await_bytes(pack_q.at[pl.ds(0, NZ * NY - 1)], out_send.at[0])
    await_bytes(landing, out_recv.at[0])
    for h in range(HEADS):
        out_ref[:, h * HD:(h + 1) * HD] = landing[h]


def local(query, key_in, value, query_gain, key_gain, tile_lists, list_lengths):
    rows, width = query.shape
    listed = tile_lists.T
    bf16 = jnp.bfloat16
    hbm = pl.BlockSpec(memory_space=pl.ANY)
    dma = pltpu.SemaphoreType.DMA
    return pl.pallas_call(
        fused_kernel,
        out_shape=jax.ShapeDtypeStruct((rows, width), bf16),
        in_specs=[hbm] * 7,
        out_specs=pl.BlockSpec(memory_space=pltpu.VMEM),
        scratch_shapes=[
            pltpu.VMEM((rows, width), bf16),
            pltpu.VMEM((rows, width), bf16),
            pltpu.VMEM((rows, width), bf16),
            pltpu.VMEM((1, width), jnp.float32),
            pltpu.VMEM((1, width), jnp.float32),
            pltpu.SMEM(listed.shape, jnp.int32),
            pltpu.SMEM(list_lengths.shape, jnp.int32),
            pltpu.VMEM((HEADS, 2, HALF, HD), bf16),
            pltpu.VMEM((HEADS, HALF, HD), bf16),
            pltpu.VMEM((BLOCKS, 2, NY, HALF, HD), bf16),
            pltpu.VMEM((BLOCKS, 2, HALF, HD), bf16),
            pltpu.VMEM((NZ * NY, HALF, HD), bf16),
            pltpu.VMEM((NZ, NY, HALF, HD), bf16),
            pltpu.VMEM((LIST, TILE, TILE), jnp.float32),
            pltpu.VMEM((UNITS, 2, HALF, HD), bf16),
            pltpu.VMEM((NZ * 2, TILE, HD), bf16),
            pltpu.VMEM((NY, NY, TILE, HD), bf16),
            pltpu.VMEM((TILE, HD), jnp.float32),
            pltpu.VMEM((NY, TILE, HD), jnp.float32),
            pltpu.VMEM((HEADS, HALF, HD), bf16),
            dma((7,)), dma((1,)), dma((2,)), dma((2,)), dma((2,)), dma((2,)), dma((2,)),
            dma((NZ,)), dma((NZ,)), dma((3, NZ)), dma((3, NZ)), dma((2,)), dma((1,)), dma((NY,)), dma((2,)), dma((1,)),
        ],
        compiler_params=pltpu.CompilerParams(
            collective_id=0, has_side_effects=True, vmem_limit_bytes=56 * 2**20
        ),
        name="fused",
    )(
        query, key_in, value, query_gain.reshape(1, -1), key_gain.reshape(1, -1),
        listed, list_lengths,
    )


def solution(mesh):
    in_specs = (
        P(("seq", "head"), None),
        P(("seq", "head"), None),
        P(("seq", "head"), None),
        P(),
        P(),
        P(),
        P(),
    )
    out_specs = P(("seq", "head"), None)
    return jax.shard_map(local, mesh=mesh, in_specs=in_specs, out_specs=out_specs, check_vma=False)
```
